32 devices in a mesh: prow: 8 (over z, y), pcol: 4 (over x, core).
Axes of the slice: x: 2, y: 2, z: 4, core: 2. Of those that a mesh axis runs over, the one named last changes fastest.
Arguments:
- right_side: bfloat16 [8, 6, 128, 256], P('prow'), may hold values from -6 to 6
- lower_inverse: bfloat16 [8, 6, 256, 256], P('prow'), as said below
- upper_inverse: bfloat16 [8, 6, 256, 256], P('prow'), as said below
- lower_blocks: bfloat16 [8, 5, 24, 256, 256], P('prow', None, 'pcol'), may hold values from -0.078125 to 0.078125
- lower_sources: int32 [8, 5, 24], P('prow', None, 'pcol'), may hold values from 0 to 39, as said below
- lower_counts: int32 [8, 5, 4], P('prow', None, 'pcol'), may hold values from 1 to 6, as said below
- upper_blocks: bfloat16 [8, 5, 24, 256, 256], P('prow', None, 'pcol'), may hold values from -0.078125 to 0.078125
- upper_sources: int32 [8, 5, 24], P('prow', None, 'pcol'), may hold values from 8 to 47, as said below
- upper_counts: int32 [8, 5, 4], P('prow', None, 'pcol'), may hold values from 1 to 6, as said below
Outputs:
- solution: bfloat16 [8, 6, 128, 256], P('prow')
The draws below stay inside these ranges and needn't reach their ends.
Inputs may be any that keep to these rules, and one draw needn't show every extreme that they name: `lower_sources`: entry [r, l, c] names supernode v * 8 + p of a level v below l + 1, with p % (4) == c // 6; entries may repeat. `upper_sources`: entry [r, l, c] names supernode v * 8 + p of a level v above l, with p % (4) == c // 6; entries may repeat. `lower_counts`: entry [r, l, g] is how many of the 6 slots of group g are live; the live ones come first. `upper_counts`: entry [r, l, g] is how many of the 6 slots of group g are live; the live ones come first. `lower_inverse`: each block is lower triangular. `upper_inverse`: each block is upper triangular.
All inputs are finite; a program needn't handle non-finite values.
Results may differ from the reference program's by a relative error of at most 0.02.
Values may be sent and summed in bfloat16 or wider, within the bound.
A program may use at most 64 MiB of HBM per device.

```python
import jax
import jax.numpy as jnp
from jax import lax

SN = 256
NRHS = 128
LEVELS = 6
BLK_DEV = 6
W = 8
BLOCKS_ROW = 24
NS = 48


def triangle_block(key, lower):
    shape = (W, LEVELS, SN, SN)
    first, second = jax.random.split(key)
    entries = jax.random.normal(first, shape, jnp.float32)
    diagonal = jnp.exp(jax.random.uniform(second, (W, LEVELS, SN), jnp.float32, -0.7, 0.7))
    rows = jnp.arange(SN, dtype=jnp.int32)[:, None]
    cols = jnp.arange(SN, dtype=jnp.int32)[None, :]
    if lower:
        keep = rows > cols
    else:
        keep = rows < cols
    off_part = jnp.where(keep, entries * SN ** (-0.5), 0.0)
    on_part = jnp.where(rows == cols, 1.0, 0.0) * diagonal[..., None]
    return off_part + on_part


def draw_lower_inverse(key, part):
    return triangle_block(jax.random.fold_in(key, 5), True).astype(jnp.bfloat16)


def draw_upper_inverse(key, part):
    return triangle_block(jax.random.fold_in(key, 6), False).astype(jnp.bfloat16)


def source_table(key, lower):
    ncol = BLOCKS_ROW // BLK_DEV
    group = W // ncol
    shape = (W, LEVELS - 1, BLOCKS_ROW)
    first, second = jax.random.split(key)
    raw = jax.random.randint(first, shape, 0, 1 << 20)
    target = jnp.arange(0, LEVELS - 1, dtype=jnp.int32)[None, :, None]
    if lower:
        level = raw % (target + 1)
    else:
        level = target + 1 + raw % (LEVELS - 1 - target)
    column = (jnp.arange(BLOCKS_ROW, dtype=jnp.int32) // BLK_DEV)[None, None, :]
    position = column + ncol * jax.random.randint(second, shape, 0, group)
    value = level * W + position
    if lower:
        value = value.at[0, 0, 0].set(0)
        value = value.at[0, LEVELS - 2, BLOCKS_ROW - 1].set((LEVELS - 1) * W - 1)
    else:
        value = value.at[0, 0, 0].set(W)
        value = value.at[0, LEVELS - 2, BLOCKS_ROW - 1].set(NS - 1)
    return value.astype(jnp.int32)


def count_table(key):
    ncol = BLOCKS_ROW // BLK_DEV
    value = jax.random.randint(key, (W, LEVELS - 1, ncol), 1, BLK_DEV + 1)
    value = value.at[0, :, 0].set(BLK_DEV)
    value = value.at[W - 1, 0, ncol - 1].set(1)
    return value.astype(jnp.int32)


def draw_lower_sources(key, part):
    return source_table(jax.random.fold_in(key, 1), True)


def draw_lower_counts(key, part):
    return count_table(jax.random.fold_in(key, 2))


def draw_upper_sources(key, part):
    return source_table(jax.random.fold_in(key, 3), False)


def draw_upper_counts(key, part):
    return count_table(jax.random.fold_in(key, 4))


def steps_of(key, extent, cuts, low, top_value):
    def one(dim, shards_of):
        heights = jax.random.uniform(jax.random.fold_in(jax.random.fold_in(key, 6), dim), (shards_of,), jnp.float32, low / len(cuts), top_value / len(cuts))
        return jnp.repeat(jnp.exp(heights), extent[dim] // shards_of).reshape((-1,) + (1,) * (len(extent) - dim - 1))

    loudness = one(*cuts[0])
    for cut in cuts[1:]:
        loudness = loudness * one(*cut)
    return loudness


def bell_draw(key, shape, width, most, pieces=(), kind=jnp.bfloat16):
    level = steps_of(key, shape, pieces, -0.22, 0.18) if pieces else 1.0
    drawn = jax.random.normal(key, shape, jnp.float32) * width * level
    return jnp.minimum(jnp.maximum(drawn, -most), most).astype(kind)


def setup_inputs(seed: int = 0) -> dict:
    arg_keys = jax.random.split(jax.random.key(seed), 10)
    return {
        "right_side": bell_draw(arg_keys[0], (W, LEVELS, NRHS, SN), 1.0, 6.0, ((0, 8),)),
        "lower_inverse": draw_lower_inverse(jax.random.fold_in(arg_keys[9], 71), 0),
        "upper_inverse": draw_upper_inverse(jax.random.fold_in(arg_keys[9], 71), 0),
        "lower_blocks": bell_draw(arg_keys[3], (W, LEVELS - 1, BLOCKS_ROW, SN, SN), (SN * BLOCKS_ROW) ** -0.5, 0.078125, ((0, 8), (2, 4))),
        "lower_sources": draw_lower_sources(jax.random.fold_in(arg_keys[9], 71), 0),
        "lower_counts": draw_lower_counts(jax.random.fold_in(arg_keys[9], 71), 0),
        "upper_blocks": bell_draw(arg_keys[6], (W, LEVELS - 1, BLOCKS_ROW, SN, SN), (SN * BLOCKS_ROW) ** -0.5, 0.078125, ((0, 8), (2, 4))),
        "upper_sources": draw_upper_sources(jax.random.fold_in(arg_keys[9], 71), 0),
        "upper_counts": draw_upper_counts(jax.random.fold_in(arg_keys[9], 71), 0),
    }


def row_update(solved, blocks, sources, counts):
    slot = jnp.arange(BLOCKS_ROW, dtype=jnp.int32)

    def one_row(args):
        row_blocks, row_sources, row_counts = args
        limit = row_counts[slot // BLK_DEV]
        live = (slot % BLK_DEV) < limit
        picked = solved[row_sources].astype(jnp.float32)
        picked = jnp.where(live[:, None, None], picked, jnp.zeros_like(picked))
        return jnp.einsum("kcb,kab->ca", picked, row_blocks.astype(jnp.float32))

    return lax.map(one_row, (blocks, sources, counts))


def apply_inverse(residual, inverse):
    return jnp.einsum("rcb,rab->rca", residual.astype(jnp.float32), inverse.astype(jnp.float32)).astype(jnp.bfloat16)


def reference(right_side, lower_inverse, upper_inverse, lower_blocks, lower_sources, lower_counts, upper_blocks, upper_sources, upper_counts):
    forward = jnp.zeros((LEVELS, W, NRHS, SN), jnp.bfloat16)
    for level in range(LEVELS):
        if level == 0:
            residual = right_side[:, 0]
        else:
            update = row_update(forward.reshape(NS, NRHS, SN), lower_blocks[:, level - 1], lower_sources[:, level - 1], lower_counts[:, level - 1])
            residual = (right_side[:, level].astype(jnp.float32) - update).astype(jnp.bfloat16)
        forward = forward.at[level].set(apply_inverse(residual, lower_inverse[:, level]))
    backward = jnp.zeros((LEVELS, W, NRHS, SN), jnp.bfloat16)
    for level in range(LEVELS - 1, -1, -1):
        if level == LEVELS - 1:
            residual = forward[level]
        else:
            update = row_update(backward.reshape(NS, NRHS, SN), upper_blocks[:, level], upper_sources[:, level], upper_counts[:, level])
            residual = (forward[level].astype(jnp.float32) - update).astype(jnp.bfloat16)
        backward = backward.at[level].set(apply_inverse(residual, upper_inverse[:, level]))
    return jnp.transpose(backward, (1, 0, 2, 3))
```

```python
import functools

import jax
import jax.numpy as jnp
from jax import lax
from jax.experimental import pallas as pl
from jax.experimental.pallas import tpu as pltpu
from jax.sharding import PartitionSpec as P

MESH = pl.DeviceIdType.MESH
NT = (((1,), (1,)), ((), ()))


def product(rows, matrix):
    return lax.dot_general(rows, matrix, NT, preferred_element_type=jnp.float32)


def kernel(
    width, ncol,
    right_hbm, linv_hbm, uinv_hbm, lblk_hbm, lsrc, lcnt, ublk_hbm, usrc, ucnt,
    out_hbm,
    right, linv, uinv, lblk, ublk, fown, bown, part, term, red, land, fstore, bstore,
    right_sem, linv_sem, uinv_sem, lblk_sem, ublk_sem,
    part_send, part_recv, cast_send, cast_recv, out_send, out_recv,
):
    levels, piece, sn = right.shape
    slots = lblk.shape[1]
    group = width // ncol
    nrhs = piece * ncol
    last = levels - 1
    p = lax.axis_index("prow")
    q = lax.axis_index("pcol")
    column = lax.rem(p, ncol)
    mine = pl.ds(pl.multiple_of(q * piece, piece), piece)

    def load_lower(l):
        return pltpu.make_async_copy(lblk_hbm.at[0, l], lblk.at[l], lblk_sem.at[l])

    def load_upper(l):
        return pltpu.make_async_copy(ublk_hbm.at[0, l], ublk.at[l], ublk_sem.at[l])

    def load_linv(l):
        return pltpu.make_async_copy(linv_hbm.at[0, l], linv.at[l], linv_sem.at[l])

    def load_uinv(l):
        return pltpu.make_async_copy(uinv_hbm.at[0, l], uinv.at[l], uinv_sem.at[l])

    load_right = pltpu.make_async_copy(right_hbm.at[0, :, mine], right, right_sem)
    load_linv(0).start()
    load_right.start()
    for l in range(last):
        load_lower(l).start()
        load_linv(l + 1).start()
    load_uinv(last).start()
    for l in range(last - 1, -1, -1):
        load_upper(l).start()
        load_uinv(l).start()

    barrier = pltpu.get_barrier_semaphore()
    for o in range(1, ncol):
        pl.semaphore_signal(barrier, inc=1, device_id=(p, lax.rem(q + o, ncol)), device_id_type=MESH)
    for g in range(group):
        row = q + g * ncol

        @pl.when(row != p)
        def _():
            for c in range(ncol):
                pl.semaphore_signal(barrier, inc=1, device_id=(row, c), device_id_type=MESH)

    fstore[levels * group] = jnp.zeros((nrhs, sn), jnp.bfloat16)
    bstore[levels * group] = jnp.zeros((nrhs, sn), jnp.bfloat16)
    pl.semaphore_wait(barrier, width + ncol - 2)

    slot_rows = pl.ds(pl.multiple_of(p // ncol * nrhs + q * piece, piece), piece)

    def cast_copy(own, l, step, row):
        return pltpu.make_async_remote_copy(
            src_ref=own.at[l], dst_ref=land.at[step, slot_rows],
            send_sem=cast_send.at[step], recv_sem=cast_recv.at[step],
            device_id=(row, column), device_id_type=MESH,
        )

    def cast(own, l, step):
        for j in range(1, width):
            cast_copy(own, l, step, lax.rem(p + j, width)).start()

        @pl.when(q != column)
        def _():
            cast_copy(own, l, step, p).start()

        @pl.when(q == column)
        def _():
            pltpu.make_async_copy(own.at[l], land.at[step, slot_rows], cast_recv.at[step]).start()

    def receive(store, l, step):
        whole = land.at[step]
        pltpu.make_async_copy(whole, whole, cast_recv.at[step]).wait()
        for g in range(group):
            store[l * group + g] = land[step, pl.ds(g * nrhs, nrhs)]

    def solve(step, at, row, right_ref, inverse, blocks, sources, counts, store, own):
        count = counts[0, at, 0]
        total = None
        for c in range(slots):
            source = sources[0, at, c]
            place = lax.div(source, width) * group + lax.div(lax.rem(source, width), ncol)
            place = jnp.where(c < count, place, levels * group)
            now = product(store[place], blocks[at, c])
            total = now if total is None else total + now
        term[...] = total
        part[step] = total.astype(jnp.bfloat16)
        for o in range(1, ncol):
            peer = lax.rem(q + o, ncol)
            pltpu.make_async_remote_copy(
                src_ref=part.at[step, pl.ds(pl.multiple_of(peer * piece, piece), piece)],
                dst_ref=red.at[step, o - 1],
                send_sem=part_send.at[step], recv_sem=part_recv.at[step],
                device_id=(p, peer), device_id_type=MESH,
            ).start()
        update = term[mine]
        arrived = red.at[step]
        pltpu.make_async_copy(arrived, arrived, part_recv.at[step]).wait()
        for o in range(ncol - 1):
            update = update + red[step, o].astype(jnp.float32)
        residual = (right_ref[row].astype(jnp.float32) - update).astype(jnp.bfloat16)
        own[row] = product(residual, inverse[row]).astype(jnp.bfloat16)

    def hand_out(l):
        place = out_hbm.at[0, l, mine]
        for o in range(1, ncol):
            pltpu.make_async_remote_copy(
                src_ref=bown.at[l], dst_ref=place,
                send_sem=out_send.at[l], recv_sem=out_recv,
                device_id=(p, lax.rem(q + o, ncol)), device_id_type=MESH,
            ).start()
        pltpu.make_async_copy(bown.at[l], place, out_recv).start()

    load_linv(0).wait()
    load_right.wait()
    fown[0] = product(right[0], linv[0]).astype(jnp.bfloat16)
    cast(fown, 0, 0)

    def forward(l, _):
        load_lower(l - 1).wait()
        load_linv(l).wait()
        receive(fstore, l - 1, l - 1)
        solve(l - 1, l - 1, l, right, linv, lblk, lsrc, lcnt, fstore, fown)

        @pl.when(l < last)
        def _():
            cast(fown, l, l)

        return 0

    lax.fori_loop(1, levels, forward, 0)

    load_uinv(last).wait()
    bown[last] = product(fown[last], uinv[last]).astype(jnp.bfloat16)
    cast(bown, last, last)
    hand_out(last)

    def backward(i, _):
        l = last - 1 - i
        step = last + i
        load_upper(l).wait()
        load_uinv(l).wait()
        receive(bstore, l + 1, step)
        solve(step, l, l, fown, uinv, ublk, usrc, ucnt, bstore, bown)

        @pl.when(l > 0)
        def _():
            cast(bown, l, step + 1)

        hand_out(l)
        return 0

    lax.fori_loop(0, last, backward, 0)

    def drain(step, _):
        sent = red.at[step]
        pltpu.make_async_copy(sent, sent, part_send.at[step]).wait()
        sent = land.at[step, pl.ds(0, (width - 1) * piece)]
        pltpu.make_async_copy(sent, sent, cast_send.at[step]).wait()

        @pl.when(q != column)
        def _():
            one = land.at[step, pl.ds(0, piece)]
            pltpu.make_async_copy(one, one, cast_send.at[step]).wait()

        return 0

    lax.fori_loop(0, 2 * last, drain, 0)
    for l in range(levels):
        sent = red.at[0]
        pltpu.make_async_copy(sent, sent, out_send.at[l]).wait()
    pltpu.make_async_copy(out_hbm.at[0], out_hbm.at[0], out_recv).wait()


def shards(right_side, lower_inverse, upper_inverse, lower_blocks, lower_sources, lower_counts,
           upper_blocks, upper_sources, upper_counts):
    width = lax.axis_size("prow")
    ncol = lax.axis_size("pcol")
    group = width // ncol
    _, levels, nrhs, sn = right_side.shape
    slots = lower_blocks.shape[2]
    piece = nrhs // ncol
    steps = 2 * (levels - 1)
    bf16 = jnp.bfloat16
    anywhere = pl.BlockSpec(memory_space=pl.ANY)
    scalars = pl.BlockSpec(memory_space=pltpu.SMEM)
    dma = pltpu.SemaphoreType.DMA
    return pl.pallas_call(
        functools.partial(kernel, width, ncol),
        out_shape=jax.ShapeDtypeStruct(right_side.shape, bf16),
        in_specs=[anywhere, anywhere, anywhere, anywhere, scalars, scalars, anywhere, scalars, scalars],
        out_specs=anywhere,
        scratch_shapes=[
            pltpu.VMEM((levels, piece, sn), bf16),
            pltpu.VMEM((levels, sn, sn), bf16),
            pltpu.VMEM((levels, sn, sn), bf16),
            pltpu.VMEM((levels - 1, slots, sn, sn), bf16),
            pltpu.VMEM((levels - 1, slots, sn, sn), bf16),
            pltpu.VMEM((levels, piece, sn), bf16),
            pltpu.VMEM((levels, piece, sn), bf16),
            pltpu.VMEM((steps, nrhs, sn), bf16),
            pltpu.VMEM((nrhs, sn), jnp.float32),
            pltpu.VMEM((steps, ncol - 1, piece, sn), bf16),
            pltpu.VMEM((steps, group * nrhs, sn), bf16),
            pltpu.VMEM((levels * group + 1, nrhs, sn), bf16),
            pltpu.VMEM((levels * group + 1, nrhs, sn), bf16),
            dma, dma((levels,)), dma((levels,)), dma((levels - 1,)), dma((levels - 1,)),
            dma((steps,)), dma((steps,)), dma((steps,)), dma((steps,)), dma((levels,)), dma,
        ],
        compiler_params=pltpu.CompilerParams(
            collective_id=0, has_side_effects=True, vmem_limit_bytes=60 * 1024 * 1024
        ),
        cost_estimate=pl.CostEstimate(flops=1200000000, bytes_accessed=10000000, transcendentals=0),
    )(right_side, lower_inverse, upper_inverse, lower_blocks, lower_sources, lower_counts,
      upper_blocks, upper_sources, upper_counts)


def solution(mesh):
    in_specs = (
        P("prow", None, None, None),
        P("prow", None, None, None),
        P("prow", None, None, None),
        P("prow", None, "pcol", None, None),
        P("prow", None, "pcol"),
        P("prow", None, "pcol"),
        P("prow", None, "pcol", None, None),
        P("prow", None, "pcol"),
        P("prow", None, "pcol"),
    )
    out_specs = P("prow", None, None, None)
    return jax.shard_map(shards, mesh=mesh, in_specs=in_specs, out_specs=out_specs, check_vma=False)
```

```python
import functools

import jax
import jax.numpy as jnp
from jax import lax
from jax.experimental import pallas as pl
from jax.experimental.pallas import tpu as pltpu
from jax.sharding import PartitionSpec as P

MESH = pl.DeviceIdType.MESH
NT = (((1,), (1,)), ((), ()))


def product(rows, matrix):
    return lax.dot_general(rows, matrix, NT, preferred_element_type=jnp.float32)


def kernel(
    width, ncol, chains,
    right_hbm, linv_hbm, uinv_hbm, lblk_hbm, lsrc, lcnt, ublk_hbm, usrc, ucnt,
    out_hbm,
    right, linv, uinv, lblk, ublk, fown, bown, part, term, red, land, fstore, bstore,
    right_sem, linv_sem, uinv_sem, lblk_sem, ublk_sem,
    part_send, part_recv, cast_send, cast_recv, out_send, out_recv,
):
    levels, piece, sn = right.shape
    slots = lblk.shape[1]
    group = width // ncol
    nrhs = piece * ncol
    rows = piece // chains
    span = nrhs // chains
    last = levels - 1
    p = lax.axis_index("prow")
    q = lax.axis_index("pcol")
    column = lax.rem(p, ncol)
    mine = pl.ds(pl.multiple_of(q * piece, piece), piece)

    def load_lower(l):
        return pltpu.make_async_copy(lblk_hbm.at[0, l], lblk.at[l], lblk_sem.at[l])

    def load_upper(l):
        return pltpu.make_async_copy(ublk_hbm.at[0, l], ublk.at[l], ublk_sem.at[l])

    def load_linv(l):
        return pltpu.make_async_copy(linv_hbm.at[0, l], linv.at[l], linv_sem.at[l])

    def load_uinv(l):
        return pltpu.make_async_copy(uinv_hbm.at[0, l], uinv.at[l], uinv_sem.at[l])

    load_right = pltpu.make_async_copy(right_hbm.at[0, :, mine], right, right_sem)
    load_linv(0).start()
    load_right.start()
    for l in range(last):
        load_lower(l).start()
        load_linv(l + 1).start()
    load_uinv(last).start()
    for l in range(last - 1, -1, -1):
        load_upper(l).start()
        load_uinv(l).start()

    barrier = pltpu.get_barrier_semaphore()
    for o in range(1, ncol):
        pl.semaphore_signal(barrier, inc=1, device_id=(p, lax.rem(q + o, ncol)), device_id_type=MESH)
    for g in range(group):
        row = q + g * ncol

        @pl.when(row != p)
        def _():
            for c in range(ncol):
                pl.semaphore_signal(barrier, inc=1, device_id=(row, c), device_id_type=MESH)

    for k in range(chains):
        fstore[k, levels * group] = jnp.zeros((span, sn), jnp.bfloat16)
        bstore[k, levels * group] = jnp.zeros((span, sn), jnp.bfloat16)
    pl.semaphore_wait(barrier, width + ncol - 2)

    slot_rows = pl.ds(pl.multiple_of(p // ncol * span + q * rows, rows), rows)

    def cast_copy(own, l, step, k, row):
        return pltpu.make_async_remote_copy(
            src_ref=own.at[l, pl.ds(k * rows, rows)], dst_ref=land.at[step, k, slot_rows],
            send_sem=cast_send.at[step], recv_sem=cast_recv.at[step, k],
            device_id=(row, column), device_id_type=MESH,
        )

    def cast(own, l, step, k):
        for j in range(1, width):
            cast_copy(own, l, step, k, lax.rem(p + j, width)).start()

        @pl.when(q != column)
        def _():
            cast_copy(own, l, step, k, p).start()

        @pl.when(q == column)
        def _():
            pltpu.make_async_copy(
                own.at[l, pl.ds(k * rows, rows)], land.at[step, k, slot_rows], cast_recv.at[step, k]
            ).start()

    def receive(store, l, step, k):
        whole = land.at[step, k]
        pltpu.make_async_copy(whole, whole, cast_recv.at[step, k]).wait()
        for g in range(group):
            store[k, l * group + g] = land[step, k, pl.ds(g * span, span)]

    def contract(step, at, k, blocks, sources, counts, store):
        count = counts[0, 0, at]
        total = None
        for c in range(slots):
            source = sources[at, 0, c]
            place = lax.div(source, width) * group + lax.div(lax.rem(source, width), ncol)
            place = jnp.where(c < count, place, levels * group)
            now = product(store[k, place], blocks[at, c])
            total = now if total is None else total + now
        part[step, k] = total.astype(jnp.bfloat16)
        for o in range(1, ncol):
            peer = lax.rem(q + o, ncol)
            pltpu.make_async_remote_copy(
                src_ref=part.at[step, k, pl.ds(pl.multiple_of(peer * rows, rows), rows)],
                dst_ref=red.at[step, k, o - 1],
                send_sem=part_send.at[step], recv_sem=part_recv.at[step, k],
                device_id=(p, peer), device_id_type=MESH,
            ).start()
        term[k] = total

    def finish(step, row, k, right_ref, inverse, own):
        update = term[k, pl.ds(pl.multiple_of(q * rows, rows), rows)]
        arrived = red.at[step, k]
        pltpu.make_async_copy(arrived, arrived, part_recv.at[step, k]).wait()
        for o in range(ncol - 1):
            update = update + red[step, k, o].astype(jnp.float32)
        here = pl.ds(k * rows, rows)
        residual = (right_ref[row, here].astype(jnp.float32) - update).astype(jnp.bfloat16)
        own[row, here] = product(residual, inverse[row]).astype(jnp.bfloat16)

    def hand_out(l):
        place = out_hbm.at[0, l, mine]
        for o in range(1, ncol):
            pltpu.make_async_remote_copy(
                src_ref=bown.at[l], dst_ref=place,
                send_sem=out_send.at[l], recv_sem=out_recv,
                device_id=(p, lax.rem(q + o, ncol)), device_id_type=MESH,
            ).start()
        pltpu.make_async_copy(bown.at[l], place, out_recv).start()

    load_linv(0).wait()
    load_right.wait()
    fown[0] = product(right[0], linv[0]).astype(jnp.bfloat16)
    for k in range(chains):
        cast(fown, 0, 0, k)

    def forward(l, _):
        load_lower(l - 1).wait()
        load_linv(l).wait()
        for k in range(chains):
            receive(fstore, l - 1, l - 1, k)
            contract(l - 1, l - 1, k, lblk, lsrc, lcnt, fstore)
        for k in range(chains):
            finish(l - 1, l, k, right, linv, fown)

            @pl.when(l < last)
            def _():
                cast(fown, l, l, k)

        return 0

    lax.fori_loop(1, levels, forward, 0)

    load_uinv(last).wait()
    bown[last] = product(fown[last], uinv[last]).astype(jnp.bfloat16)
    for k in range(chains):
        cast(bown, last, last, k)
    hand_out(last)

    def backward(i, _):
        l = last - 1 - i
        step = last + i
        load_upper(l).wait()
        load_uinv(l).wait()
        for k in range(chains):
            receive(bstore, l + 1, step, k)
            contract(step, l, k, ublk, usrc, ucnt, bstore)
        for k in range(chains):
            finish(step, l, k, fown, uinv, bown)

            @pl.when(l > 0)
            def _():
                cast(bown, l, step + 1, k)

        hand_out(l)
        return 0

    lax.fori_loop(0, last, backward, 0)

    def drain(step, _):
        sent = red.at[step]
        pltpu.make_async_copy(sent, sent, part_send.at[step]).wait()
        for k in range(chains):
            sent = land.at[step, k, pl.ds(0, (width - 1) * rows)]
            pltpu.make_async_copy(sent, sent, cast_send.at[step]).wait()

        @pl.when(q != column)
        def _():
            one = land.at[step, 0, pl.ds(0, piece)]
            pltpu.make_async_copy(one, one, cast_send.at[step]).wait()

        return 0

    lax.fori_loop(0, 2 * last, drain, 0)
    for l in range(levels):
        sent = red.at[0]
        pltpu.make_async_copy(sent, sent, out_send.at[l]).wait()
    pltpu.make_async_copy(out_hbm.at[0], out_hbm.at[0], out_recv).wait()


def shards(right_side, lower_inverse, upper_inverse, lower_blocks, lower_sources, lower_counts,
           upper_blocks, upper_sources, upper_counts):
    width = lax.axis_size("prow")
    ncol = lax.axis_size("pcol")
    group = width // ncol
    _, levels, nrhs, sn = right_side.shape
    slots = lower_blocks.shape[2]
    piece = nrhs // ncol
    chains = 2 if piece % 32 == 0 else 1
    steps = 2 * (levels - 1)
    bf16 = jnp.bfloat16
    anywhere = pl.BlockSpec(memory_space=pl.ANY)
    scalars = pl.BlockSpec(memory_space=pltpu.SMEM)
    dma = pltpu.SemaphoreType.DMA
    return pl.pallas_call(
        functools.partial(kernel, width, ncol, chains),
        out_shape=jax.ShapeDtypeStruct(right_side.shape, bf16),
        in_specs=[anywhere, anywhere, anywhere, anywhere, scalars, scalars, anywhere, scalars, scalars],
        out_specs=anywhere,
        scratch_shapes=[
            pltpu.VMEM((levels, piece, sn), bf16),
            pltpu.VMEM((levels, sn, sn), bf16),
            pltpu.VMEM((levels, sn, sn), bf16),
            pltpu.VMEM((levels - 1, slots, sn, sn), bf16),
            pltpu.VMEM((levels - 1, slots, sn, sn), bf16),
            pltpu.VMEM((levels, piece, sn), bf16),
            pltpu.VMEM((levels, piece, sn), bf16),
            pltpu.VMEM((steps, chains, nrhs // chains, sn), bf16),
            pltpu.VMEM((chains, nrhs // chains, sn), jnp.float32),
            pltpu.VMEM((steps, chains, ncol - 1, piece // chains, sn), bf16),
            pltpu.VMEM((steps, chains, group * nrhs // chains, sn), bf16),
            pltpu.VMEM((chains, levels * group + 1, nrhs // chains, sn), bf16),
            pltpu.VMEM((chains, levels * group + 1, nrhs // chains, sn), bf16),
            dma, dma((levels,)), dma((levels,)), dma((levels - 1,)), dma((levels - 1,)),
            dma((steps,)), dma((steps, chains)), dma((steps,)), dma((steps, chains)), dma((levels,)), dma,
        ],
        compiler_params=pltpu.CompilerParams(
            collective_id=0, has_side_effects=True, vmem_limit_bytes=60 * 1024 * 1024
        ),
        cost_estimate=pl.CostEstimate(flops=1200000000, bytes_accessed=10000000, transcendentals=0),
    )(right_side, lower_inverse, upper_inverse,
      lower_blocks, jnp.swapaxes(lower_sources, 0, 1), jnp.swapaxes(lower_counts, 1, 2),
      upper_blocks, jnp.swapaxes(upper_sources, 0, 1), jnp.swapaxes(upper_counts, 1, 2))


def solution(mesh):
    in_specs = (
        P("prow", None, None, None),
        P("prow", None, None, None),
        P("prow", None, None, None),
        P("prow", None, "pcol", None, None),
        P("prow", None, "pcol"),
        P("prow", None, "pcol"),
        P("prow", None, "pcol", None, None),
        P("prow", None, "pcol"),
        P("prow", None, "pcol"),
    )
    out_specs = P("prow", None, None, None)
    return jax.shard_map(shards, mesh=mesh, in_specs=in_specs, out_specs=out_specs, check_vma=False)
```

```python
import functools

import jax
import jax.numpy as jnp
from jax import lax
from jax.experimental import pallas as pl
from jax.experimental.pallas import tpu as pltpu
from jax.sharding import PartitionSpec as P

MESH = pl.DeviceIdType.MESH
NT = (((1,), (1,)), ((), ()))


def product(rows, matrix):
    return lax.dot_general(rows, matrix, NT, preferred_element_type=jnp.float32)


def kernel(
    width, ncol, inner, chains,
    right_hbm, linv_hbm, uinv_hbm, lblk_hbm, lsrc, lcnt, ublk_hbm, usrc, ucnt,
    out_hbm,
    right, linv, uinv, lblk, ublk, fown, bown, part, term, red, hop, land, fstore, bstore,
    right_sem, linv_sem, uinv_sem, lblk_sem, ublk_sem,
    part_send, part_recv, cast_send, hop_recv, cast_recv, out_send, out_recv,
):
    levels, piece, sn = right.shape
    slots = lblk.shape[1]
    group = width // ncol
    nrhs = piece * ncol
    rows = piece // chains
    span = nrhs // chains
    last = levels - 1
    p = lax.axis_index("prow")
    q = lax.axis_index("pcol")
    outer = width // inner
    p_out = lax.div(p, inner)
    p_in = lax.rem(p, inner)
    mine = pl.ds(pl.multiple_of(q * piece, piece), piece)

    def load_lower(l):
        return pltpu.make_async_copy(lblk_hbm.at[0, l], lblk.at[l], lblk_sem.at[l])

    def load_upper(l):
        return pltpu.make_async_copy(ublk_hbm.at[0, l], ublk.at[l], ublk_sem.at[l])

    def load_linv(l):
        return pltpu.make_async_copy(linv_hbm.at[0, l], linv.at[l], linv_sem.at[l])

    def load_uinv(l):
        return pltpu.make_async_copy(uinv_hbm.at[0, l], uinv.at[l], uinv_sem.at[l])

    load_right = pltpu.make_async_copy(right_hbm.at[0, :, mine], right, right_sem)
    load_linv(0).start()
    load_right.start()
    for l in range(last):
        load_lower(l).start()
        load_linv(l + 1).start()
    load_uinv(last).start()
    for l in range(last - 1, -1, -1):
        load_upper(l).start()
        load_uinv(l).start()

    barrier = pltpu.get_barrier_semaphore()

    def greet(row, c):
        pl.semaphore_signal(barrier, inc=1, device_id=(row, c), device_id_type=MESH)

    for o in range(1, outer):
        greet(lax.rem(p_out + o, outer) * inner + p_in, q)
    for i in range(inner):
        for o in range(0 if i else 1, ncol):
            greet(p_out * inner + lax.rem(p_in + i, inner), lax.rem(q + o, ncol))

    for k in range(chains):
        fstore[k, levels * group] = jnp.zeros((span, sn), jnp.bfloat16)
        bstore[k, levels * group] = jnp.zeros((span, sn), jnp.bfloat16)
    pl.semaphore_wait(barrier, outer + inner * ncol - 2)

    low = p_out < outer // 2
    edge = jnp.where(low, p_out, outer - 1 - p_out)

    def layer(i):
        at = jnp.where(i >= edge, i + 1, i)
        return jnp.where(low, at, outer - 1 - at)

    def forward_piece(piece_ref, step, k, z):
        origin = z * inner + p_in
        column = lax.rem(origin, ncol)
        start = lax.div(origin, ncol) * span + q * rows
        place = land.at[step, k, pl.ds(pl.multiple_of(start, rows), rows)]

        def send(row):
            pltpu.make_async_remote_copy(
                src_ref=piece_ref, dst_ref=place,
                send_sem=cast_send.at[step], recv_sem=cast_recv.at[step, k],
                device_id=(row, column), device_id_type=MESH,
            ).start()

        for i in range(1, inner):
            send(p_out * inner + lax.rem(p_in + i, inner))

        @pl.when(q != column)
        def _():
            send(p)

        @pl.when(q == column)
        def _():
            pltpu.make_async_copy(piece_ref, place, cast_recv.at[step, k]).start()

    def cast(own, l, step, k):
        piece_ref = own.at[l, pl.ds(k * rows, rows)]
        for i in range(outer - 2, -1, -1):
            pltpu.make_async_remote_copy(
                src_ref=piece_ref, dst_ref=hop.at[step, k, p_out],
                send_sem=cast_send.at[step], recv_sem=hop_recv.at[step, k, p_out],
                device_id=(layer(i) * inner + p_in, q), device_id_type=MESH,
            ).start()
        forward_piece(piece_ref, step, k, p_out)

    def relay(step, k):
        for i in range(outer - 1):
            z = layer(i)
            arrived = hop.at[step, k, z]
            pltpu.make_async_copy(arrived, arrived, hop_recv.at[step, k, z]).wait()
            forward_piece(arrived, step, k, z)

    def receive(store, l, step, k):
        whole = land.at[step, k]
        pltpu.make_async_copy(whole, whole, cast_recv.at[step, k]).wait()
        for g in range(group):
            store[k, l * group + g] = land[step, k, pl.ds(g * span, span)]

    def contract(step, at, k, blocks, sources, counts, store):
        count = counts[0, 0, at]
        total = None
        for c in range(slots):
            source = sources[at, 0, c]
            place = lax.div(source, width) * group + lax.div(lax.rem(source, width), ncol)
            place = jnp.where(c < count, place, levels * group)
            now = product(store[k, place], blocks[at, c])
            total = now if total is None else total + now
        part[step, k] = total.astype(jnp.bfloat16)
        for o in range(1, ncol):
            peer = lax.rem(q + o, ncol)
            pltpu.make_async_remote_copy(
                src_ref=part.at[step, k, pl.ds(pl.multiple_of(peer * rows, rows), rows)],
                dst_ref=red.at[step, k, o - 1],
                send_sem=part_send.at[step], recv_sem=part_recv.at[step, k],
                device_id=(p, peer), device_id_type=MESH,
            ).start()
        term[k] = total

    def finish(step, row, k, right_ref, inverse, own):
        update = term[k, pl.ds(pl.multiple_of(q * rows, rows), rows)]
        arrived = red.at[step, k]
        pltpu.make_async_copy(arrived, arrived, part_recv.at[step, k]).wait()
        for o in range(ncol - 1):
            update = update + red[step, k, o].astype(jnp.float32)
        here = pl.ds(k * rows, rows)
        residual = (right_ref[row, here].astype(jnp.float32) - update).astype(jnp.bfloat16)
        own[row, here] = product(residual, inverse[row]).astype(jnp.bfloat16)

    def hand_out(l):
        place = out_hbm.at[0, l, mine]
        for o in range(1, ncol):
            pltpu.make_async_remote_copy(
                src_ref=bown.at[l], dst_ref=place,
                send_sem=out_send.at[l], recv_sem=out_recv,
                device_id=(p, lax.rem(q + o, ncol)), device_id_type=MESH,
            ).start()
        pltpu.make_async_copy(bown.at[l], place, out_recv).start()

    load_linv(0).wait()
    load_right.wait()
    fown[0] = product(right[0], linv[0]).astype(jnp.bfloat16)
    for k in range(chains):
        cast(fown, 0, 0, k)

    def forward(l, _):
        load_lower(l - 1).wait()
        load_linv(l).wait()
        for k in range(chains):
            relay(l - 1, k)
        for k in range(chains):
            receive(fstore, l - 1, l - 1, k)
            contract(l - 1, l - 1, k, lblk, lsrc, lcnt, fstore)
        for k in range(chains):
            finish(l - 1, l, k, right, linv, fown)

            @pl.when(l < last)
            def _():
                cast(fown, l, l, k)

        return 0

    lax.fori_loop(1, levels, forward, 0)

    load_uinv(last).wait()
    bown[last] = product(fown[last], uinv[last]).astype(jnp.bfloat16)
    for k in range(chains):
        cast(bown, last, last, k)
    hand_out(last)

    def backward(i, _):
        l = last - 1 - i
        step = last + i
        load_upper(l).wait()
        load_uinv(l).wait()
        for k in range(chains):
            relay(step, k)
        for k in range(chains):
            receive(bstore, l + 1, step, k)
            contract(step, l, k, ublk, usrc, ucnt, bstore)
        for k in range(chains):
            finish(step, l, k, fown, uinv, bown)

            @pl.when(l > 0)
            def _():
                cast(bown, l, step + 1, k)

        hand_out(l)
        return 0

    lax.fori_loop(0, last, backward, 0)

    def drain(step, _):
        sent = red.at[step]
        pltpu.make_async_copy(sent, sent, part_send.at[step]).wait()
        for k in range(chains):
            sent = land.at[step, k, pl.ds(0, (width - 1) * rows)]
            pltpu.make_async_copy(sent, sent, cast_send.at[step]).wait()

        for z in range(outer):

            @pl.when(q != lax.rem(z * inner + p_in, ncol))
            def _():
                one = land.at[step, 0, pl.ds(0, piece)]
                pltpu.make_async_copy(one, one, cast_send.at[step]).wait()

        return 0

    lax.fori_loop(0, 2 * last, drain, 0)
    for l in range(levels):
        sent = red.at[0]
        pltpu.make_async_copy(sent, sent, out_send.at[l]).wait()
    pltpu.make_async_copy(out_hbm.at[0], out_hbm.at[0], out_recv).wait()


def shards(right_side, lower_inverse, upper_inverse, lower_blocks, lower_sources, lower_counts,
           upper_blocks, upper_sources, upper_counts):
    width = lax.axis_size("prow")
    ncol = lax.axis_size("pcol")
    group = width // ncol
    _, levels, nrhs, sn = right_side.shape
    slots = lower_blocks.shape[2]
    piece = nrhs // ncol
    chains = 2 if piece % 32 == 0 else 1
    inner = 1
    while inner * inner * 4 <= width:
        inner *= 2
    steps = 2 * (levels - 1)
    bf16 = jnp.bfloat16
    anywhere = pl.BlockSpec(memory_space=pl.ANY)
    scalars = pl.BlockSpec(memory_space=pltpu.SMEM)
    dma = pltpu.SemaphoreType.DMA
    return pl.pallas_call(
        functools.partial(kernel, width, ncol, inner, chains),
        out_shape=jax.ShapeDtypeStruct(right_side.shape, bf16),
        in_specs=[anywhere, anywhere, anywhere, anywhere, scalars, scalars, anywhere, scalars, scalars],
        out_specs=anywhere,
        scratch_shapes=[
            pltpu.VMEM((levels, piece, sn), bf16),
            pltpu.VMEM((levels, sn, sn), bf16),
            pltpu.VMEM((levels, sn, sn), bf16),
            pltpu.VMEM((levels - 1, slots, sn, sn), bf16),
            pltpu.VMEM((levels - 1, slots, sn, sn), bf16),
            pltpu.VMEM((levels, piece, sn), bf16),
            pltpu.VMEM((levels, piece, sn), bf16),
            pltpu.VMEM((steps, chains, nrhs // chains, sn), bf16),
            pltpu.VMEM((chains, nrhs // chains, sn), jnp.float32),
            pltpu.VMEM((steps, chains, ncol - 1, piece // chains, sn), bf16),
            pltpu.VMEM((steps, chains, width // inner, piece // chains, sn), bf16),
            pltpu.VMEM((steps, chains, group * nrhs // chains, sn), bf16),
            pltpu.VMEM((chains, levels * group + 1, nrhs // chains, sn), bf16),
            pltpu.VMEM((chains, levels * group + 1, nrhs // chains, sn), bf16),
            dma, dma((levels,)), dma((levels,)), dma((levels - 1,)), dma((levels - 1,)),
            dma((steps,)), dma((steps, chains)), dma((steps,)), dma((steps, chains, width // inner)), dma((steps, chains)), dma((levels,)), dma,
        ],
        compiler_params=pltpu.CompilerParams(
            collective_id=0, has_side_effects=True, vmem_limit_bytes=60 * 1024 * 1024
        ),
        cost_estimate=pl.CostEstimate(flops=1200000000, bytes_accessed=10000000, transcendentals=0),
    )(right_side, lower_inverse, upper_inverse,
      lower_blocks, jnp.swapaxes(lower_sources, 0, 1), jnp.swapaxes(lower_counts, 1, 2),
      upper_blocks, jnp.swapaxes(upper_sources, 0, 1), jnp.swapaxes(upper_counts, 1, 2))


def solution(mesh):
    in_specs = (
        P("prow", None, None, None),
        P("prow", None, None, None),
        P("prow", None, None, None),
        P("prow", None, "pcol", None, None),
        P("prow", None, "pcol"),
        P("prow", None, "pcol"),
        P("prow", None, "pcol", None, None),
        P("prow", None, "pcol"),
        P("prow", None, "pcol"),
    )
    out_specs = P("prow", None, None, None)
    return jax.shard_map(shards, mesh=mesh, in_specs=in_specs, out_specs=out_specs, check_vma=False)
```

```python
import functools

import jax
import jax.numpy as jnp
from jax import lax
from jax.experimental import pallas as pl
from jax.experimental.pallas import tpu as pltpu
from jax.sharding import PartitionSpec as P

MESH = pl.DeviceIdType.MESH
NT = (((1,), (1,)), ((), ()))


def product(rows, matrix):
    return lax.dot_general(rows, matrix, NT, preferred_element_type=jnp.float32)


def kernel(
    width, ncol, chains,
    right_hbm, linv_hbm, uinv_hbm, lblk_hbm, lsrc, lcnt, ublk_hbm, usrc, ucnt,
    out_hbm,
    right, linv, uinv, lblk, ublk, fown, bown, part, term, red, land, fstore, bstore, sums, past,
    right_sem, linv_sem, uinv_sem, lblk_sem, ublk_sem,
    part_send, part_recv, cast_send, cast_recv, out_send, out_recv,
):
    levels, piece, sn = right.shape
    slots = lblk.shape[1]
    group = width // ncol
    nrhs = piece * ncol
    rows = piece // chains
    span = nrhs // chains
    last = levels - 1
    p = lax.axis_index("prow")
    q = lax.axis_index("pcol")
    column = lax.rem(p, ncol)
    mine = pl.ds(pl.multiple_of(q * piece, piece), piece)

    def load_lower(l):
        return pltpu.make_async_copy(lblk_hbm.at[0, l], lblk.at[l], lblk_sem.at[l])

    def load_upper(l):
        return pltpu.make_async_copy(ublk_hbm.at[0, l], ublk.at[l], ublk_sem.at[l])

    def load_linv(l):
        return pltpu.make_async_copy(linv_hbm.at[0, l], linv.at[l], linv_sem.at[l])

    def load_uinv(l):
        return pltpu.make_async_copy(uinv_hbm.at[0, l], uinv.at[l], uinv_sem.at[l])

    load_right = pltpu.make_async_copy(right_hbm.at[0, :, mine], right, right_sem)
    load_linv(0).start()
    load_right.start()
    for l in range(last):
        load_lower(l).start()
        load_linv(l + 1).start()
    load_uinv(last).start()
    for l in range(last - 1, -1, -1):
        load_upper(l).start()
        load_uinv(l).start()

    barrier = pltpu.get_barrier_semaphore()
    for o in range(1, ncol):
        pl.semaphore_signal(barrier, inc=1, device_id=(p, lax.rem(q + o, ncol)), device_id_type=MESH)
    for g in range(group):
        row = q + g * ncol

        @pl.when(row != p)
        def _():
            for c in range(ncol):
                pl.semaphore_signal(barrier, inc=1, device_id=(row, c), device_id_type=MESH)

    fstore[levels * group] = jnp.zeros((nrhs, sn), jnp.bfloat16)
    bstore[levels * group] = jnp.zeros((nrhs, sn), jnp.bfloat16)
    past[...] = jnp.zeros_like(past)
    pl.semaphore_wait(barrier, width + ncol - 2)

    slot_rows = pl.ds(pl.multiple_of(p // ncol * span + q * rows, rows), rows)

    def cast_copy(own, l, step, k, row):
        return pltpu.make_async_remote_copy(
            src_ref=own.at[l, pl.ds(k * rows, rows)], dst_ref=land.at[step, k, slot_rows],
            send_sem=cast_send.at[step], recv_sem=cast_recv.at[step, k],
            device_id=(row, column), device_id_type=MESH,
        )

    def cast(own, l, step, k):
        for j in range(1, width):
            cast_copy(own, l, step, k, lax.rem(p + j, width)).start()

        @pl.when(q != column)
        def _():
            cast_copy(own, l, step, k, p).start()

        @pl.when(q == column)
        def _():
            pltpu.make_async_copy(
                own.at[l, pl.ds(k * rows, rows)], land.at[step, k, slot_rows], cast_recv.at[step, k]
            ).start()

    def keep(store, l, step):
        for k in range(chains):
            for g in range(group):
                store[l * group + g, pl.ds(k * span, span)] = land[step, k, pl.ds(g * span, span)]

    def gather_newest(at, newest, blocks, sources, counts):
        count = counts[0, 0, at]
        weights = []
        for c in range(slots):
            source = sources[at, 0, c]
            fits = jnp.logical_and(c < count, lax.div(source, width) == newest)
            place = jnp.where(fits, lax.div(lax.rem(source, width), ncol), group)
            weights.append([jnp.where(place == g, 1.0, 0.0).astype(jnp.float32) for g in range(group)])
        height = sn // 4
        for r in range(0, sn, height):
            total = [None] * group
            for c in range(slots):
                block = blocks[at, c, pl.ds(r, height)].astype(jnp.float32)
                for g in range(group):
                    now = block * weights[c][g]
                    total[g] = now if total[g] is None else total[g] + now
            for g in range(group):
                sums[g, pl.ds(r, height)] = total[g].astype(jnp.bfloat16)

    def add_older(at, newest, blocks, sources, counts, store):
        count = counts[0, 0, at]
        total = None
        for c in range(slots):
            source = sources[at, 0, c]
            level = lax.div(source, width)
            place = level * group + lax.div(lax.rem(source, width), ncol)
            fits = jnp.logical_and(c < count, level != newest)
            now = product(store[jnp.where(fits, place, levels * group)], blocks[at, c])
            total = now if total is None else total + now
        past[...] = total

    def contract(step, k):
        whole = land.at[step, k]
        pltpu.make_async_copy(whole, whole, cast_recv.at[step, k]).wait()
        total = past[pl.ds(k * span, span)]
        for g in range(group):
            total = total + product(land[step, k, pl.ds(g * span, span)], sums[g])
        part[step, k] = total.astype(jnp.bfloat16)
        for o in range(1, ncol):
            peer = lax.rem(q + o, ncol)
            pltpu.make_async_remote_copy(
                src_ref=part.at[step, k, pl.ds(pl.multiple_of(peer * rows, rows), rows)],
                dst_ref=red.at[step, k, o - 1],
                send_sem=part_send.at[step], recv_sem=part_recv.at[step, k],
                device_id=(p, peer), device_id_type=MESH,
            ).start()
        term[k] = total

    def finish(step, row, k, right_ref, inverse, own):
        update = term[k, pl.ds(pl.multiple_of(q * rows, rows), rows)]
        arrived = red.at[step, k]
        pltpu.make_async_copy(arrived, arrived, part_recv.at[step, k]).wait()
        for o in range(ncol - 1):
            update = update + red[step, k, o].astype(jnp.float32)
        here = pl.ds(k * rows, rows)
        residual = (right_ref[row, here].astype(jnp.float32) - update).astype(jnp.bfloat16)
        own[row, here] = product(residual, inverse[row]).astype(jnp.bfloat16)

    def hand_out(l):
        place = out_hbm.at[0, l, mine]
        for o in range(1, ncol):
            pltpu.make_async_remote_copy(
                src_ref=bown.at[l], dst_ref=place,
                send_sem=out_send.at[l], recv_sem=out_recv,
                device_id=(p, lax.rem(q + o, ncol)), device_id_type=MESH,
            ).start()
        pltpu.make_async_copy(bown.at[l], place, out_recv).start()

    load_linv(0).wait()
    load_right.wait()
    fown[0] = product(right[0], linv[0]).astype(jnp.bfloat16)
    for k in range(chains):
        cast(fown, 0, 0, k)
    load_lower(0).wait()
    gather_newest(0, 0, lblk, lsrc, lcnt)

    def forward(l, _):
        for k in range(chains):
            contract(l - 1, k)

        @pl.when(l < last)
        def _():
            load_lower(l).wait()
            gather_newest(l, l, lblk, lsrc, lcnt)
            keep(fstore, l - 1, l - 1)

        load_linv(l).wait()
        for k in range(chains):
            finish(l - 1, l, k, right, linv, fown)

            @pl.when(l < last)
            def _():
                cast(fown, l, l, k)

        @pl.when(l < last)
        def _():
            add_older(l, l, lblk, lsrc, lcnt, fstore)

        return 0

    lax.fori_loop(1, levels, forward, 0)

    load_uinv(last).wait()
    bown[last] = product(fown[last], uinv[last]).astype(jnp.bfloat16)
    for k in range(chains):
        cast(bown, last, last, k)
    hand_out(last)
    load_upper(last - 1).wait()
    gather_newest(last - 1, last, ublk, usrc, ucnt)
    past[...] = jnp.zeros_like(past)

    def backward(i, _):
        l = last - 1 - i
        step = last + i
        for k in range(chains):
            contract(step, k)

        @pl.when(l > 0)
        def _():
            load_upper(l - 1).wait()
            gather_newest(l - 1, l, ublk, usrc, ucnt)
            keep(bstore, l + 1, step)

        load_uinv(l).wait()
        for k in range(chains):
            finish(step, l, k, fown, uinv, bown)

            @pl.when(l > 0)
            def _():
                cast(bown, l, step + 1, k)

        hand_out(l)

        @pl.when(l > 0)
        def _():
            add_older(l - 1, l, ublk, usrc, ucnt, bstore)

        return 0

    lax.fori_loop(0, last, backward, 0)

    def drain(step, _):
        sent = red.at[step]
        pltpu.make_async_copy(sent, sent, part_send.at[step]).wait()
        for k in range(chains):
            sent = land.at[step, k, pl.ds(0, (width - 1) * rows)]
            pltpu.make_async_copy(sent, sent, cast_send.at[step]).wait()

        @pl.when(q != column)
        def _():
            one = land.at[step, 0, pl.ds(0, piece)]
            pltpu.make_async_copy(one, one, cast_send.at[step]).wait()

        return 0

    lax.fori_loop(0, 2 * last, drain, 0)
    for l in range(levels):
        sent = red.at[0]
        pltpu.make_async_copy(sent, sent, out_send.at[l]).wait()
    pltpu.make_async_copy(out_hbm.at[0], out_hbm.at[0], out_recv).wait()


def shards(right_side, lower_inverse, upper_inverse, lower_blocks, lower_sources, lower_counts,
           upper_blocks, upper_sources, upper_counts):
    width = lax.axis_size("prow")
    ncol = lax.axis_size("pcol")
    group = width // ncol
    _, levels, nrhs, sn = right_side.shape
    slots = lower_blocks.shape[2]
    piece = nrhs // ncol
    chains = 2 if piece % 32 == 0 else 1
    steps = 2 * (levels - 1)
    bf16 = jnp.bfloat16
    anywhere = pl.BlockSpec(memory_space=pl.ANY)
    scalars = pl.BlockSpec(memory_space=pltpu.SMEM)
    dma = pltpu.SemaphoreType.DMA
    return pl.pallas_call(
        functools.partial(kernel, width, ncol, chains),
        out_shape=jax.ShapeDtypeStruct(right_side.shape, bf16),
        in_specs=[anywhere, anywhere, anywhere, anywhere, scalars, scalars, anywhere, scalars, scalars],
        out_specs=anywhere,
        scratch_shapes=[
            pltpu.VMEM((levels, piece, sn), bf16),
            pltpu.VMEM((levels, sn, sn), bf16),
            pltpu.VMEM((levels, sn, sn), bf16),
            pltpu.VMEM((levels - 1, slots, sn, sn), bf16),
            pltpu.VMEM((levels - 1, slots, sn, sn), bf16),
            pltpu.VMEM((levels, piece, sn), bf16),
            pltpu.VMEM((levels, piece, sn), bf16),
            pltpu.VMEM((steps, chains, nrhs // chains, sn), bf16),
            pltpu.VMEM((chains, nrhs // chains, sn), jnp.float32),
            pltpu.VMEM((steps, chains, ncol - 1, piece // chains, sn), bf16),
            pltpu.VMEM((steps, chains, group * nrhs // chains, sn), bf16),
            pltpu.VMEM((levels * group + 1, nrhs, sn), bf16),
            pltpu.VMEM((levels * group + 1, nrhs, sn), bf16),
            pltpu.VMEM((group, sn, sn), bf16),
            pltpu.VMEM((nrhs, sn), jnp.float32),
            dma, dma((levels,)), dma((levels,)), dma((levels - 1,)), dma((levels - 1,)),
            dma((steps,)), dma((steps, chains)), dma((steps,)), dma((steps, chains)), dma((levels,)), dma,
        ],
        compiler_params=pltpu.CompilerParams(
            collective_id=0, has_side_effects=True, vmem_limit_bytes=60 * 1024 * 1024
        ),
        cost_estimate=pl.CostEstimate(flops=1200000000, bytes_accessed=10000000, transcendentals=0),
    )(right_side, lower_inverse, upper_inverse,
      lower_blocks, jnp.swapaxes(lower_sources, 0, 1), jnp.swapaxes(lower_counts, 1, 2),
      upper_blocks, jnp.swapaxes(upper_sources, 0, 1), jnp.swapaxes(upper_counts, 1, 2))


def solution(mesh):
    in_specs = (
        P("prow", None, None, None),
        P("prow", None, None, None),
        P("prow", None, None, None),
        P("prow", None, "pcol", None, None),
        P("prow", None, "pcol"),
        P("prow", None, "pcol"),
        P("prow", None, "pcol", None, None),
        P("prow", None, "pcol"),
        P("prow", None, "pcol"),
    )
    out_specs = P("prow", None, None, None)
    return jax.shard_map(shards, mesh=mesh, in_specs=in_specs, out_specs=out_specs, check_vma=False)
```

```python
import functools

import jax
import jax.numpy as jnp
from jax import lax
from jax.experimental import pallas as pl
from jax.experimental.pallas import tpu as pltpu
from jax.sharding import PartitionSpec as P

MESH = pl.DeviceIdType.MESH
NT = (((1,), (1,)), ((), ()))


def product(rows, matrix):
    return lax.dot_general(rows, matrix, NT, preferred_element_type=jnp.float32)


def kernel(
    width, ncol, chains,
    right_hbm, linv_hbm, uinv_hbm, lblk_hbm, lsrc, lcnt, ublk_hbm, usrc, ucnt,
    out_hbm,
    right, linv, uinv, lblk, ublk, fown, bown, part, term, red, land, fstore, bstore, sums, past,
    right_sem, linv_sem, uinv_sem, lblk_sem, ublk_sem,
    part_send, part_recv, cast_send, cast_recv, out_send, out_recv,
):
    levels, piece, sn = right.shape
    slots = lblk.shape[1]
    group = width // ncol
    nrhs = piece * ncol
    rows = piece // chains
    span = nrhs // chains
    last = levels - 1
    p = lax.axis_index("prow")
    q = lax.axis_index("pcol")
    column = lax.rem(p, ncol)
    mine = pl.ds(pl.multiple_of(q * piece, piece), piece)

    def load_lower(l):
        return pltpu.make_async_copy(lblk_hbm.at[0, l], lblk.at[l], lblk_sem.at[l])

    def load_upper(l):
        return pltpu.make_async_copy(ublk_hbm.at[0, l], ublk.at[l], ublk_sem.at[l])

    def load_linv(l):
        return pltpu.make_async_copy(linv_hbm.at[0, l], linv.at[l], linv_sem.at[l])

    def load_uinv(l):
        return pltpu.make_async_copy(uinv_hbm.at[0, l], uinv.at[l], uinv_sem.at[l])

    load_right = pltpu.make_async_copy(right_hbm.at[0, :, mine], right, right_sem)
    load_linv(0).start()
    load_right.start()
    for l in range(last):
        load_lower(l).start()
        load_linv(l + 1).start()
    load_uinv(last).start()
    for l in range(last - 1, -1, -1):
        load_upper(l).start()
        load_uinv(l).start()

    barrier = pltpu.get_barrier_semaphore()
    for o in range(1, ncol):
        pl.semaphore_signal(barrier, inc=1, device_id=(p, lax.rem(q + o, ncol)), device_id_type=MESH)
    for g in range(group):
        row = q + g * ncol

        @pl.when(row != p)
        def _():
            for c in range(ncol):
                pl.semaphore_signal(barrier, inc=1, device_id=(row, c), device_id_type=MESH)

    for k in range(chains):
        fstore[k, levels * group] = jnp.zeros((span, sn), jnp.bfloat16)
        bstore[k, levels * group] = jnp.zeros((span, sn), jnp.bfloat16)
    past[...] = jnp.zeros_like(past)
    pl.semaphore_wait(barrier, width + ncol - 2)

    slot_rows = pl.ds(pl.multiple_of(p // ncol * span + q * rows, rows), rows)

    def cast_copy(own, l, step, k, row):
        return pltpu.make_async_remote_copy(
            src_ref=own.at[l, pl.ds(k * rows, rows)], dst_ref=land.at[step, k, slot_rows],
            send_sem=cast_send.at[step], recv_sem=cast_recv.at[step, k],
            device_id=(row, column), device_id_type=MESH,
        )

    def cast(own, l, step, k):
        for j in range(1, width):
            cast_copy(own, l, step, k, lax.rem(p + j, width)).start()

        @pl.when(q != column)
        def _():
            cast_copy(own, l, step, k, p).start()

        @pl.when(q == column)
        def _():
            pltpu.make_async_copy(
                own.at[l, pl.ds(k * rows, rows)], land.at[step, k, slot_rows], cast_recv.at[step, k]
            ).start()

    def keep(store, l, step, k):
        for g in range(group):
            store[k, l * group + g] = land[step, k, pl.ds(g * span, span)]

    def gather_newest(at, newest, blocks, sources, counts):
        count = counts[0, 0, at]
        weights = []
        for c in range(slots):
            source = sources[at, 0, c]
            fits = jnp.logical_and(c < count, lax.div(source, width) == newest)
            place = jnp.where(fits, lax.div(lax.rem(source, width), ncol), group)
            weights.append([jnp.where(place == g, 1.0, 0.0).astype(jnp.float32) for g in range(group)])
        height = sn // 4
        for r in range(0, sn, height):
            total = [None] * group
            for c in range(slots):
                block = blocks[at, c, pl.ds(r, height)].astype(jnp.float32)
                for g in range(group):
                    now = block * weights[c][g]
                    total[g] = now if total[g] is None else total[g] + now
            for g in range(group):
                sums[g, pl.ds(r, height)] = total[g].astype(jnp.bfloat16)

    def add_older(at, newest, k, blocks, sources, counts, store):
        count = counts[0, 0, at]
        total = None
        for c in range(slots):
            source = sources[at, 0, c]
            level = lax.div(source, width)
            place = level * group + lax.div(lax.rem(source, width), ncol)
            fits = jnp.logical_and(c < count, level != newest)
            now = product(store[k, jnp.where(fits, place, levels * group)], blocks[at, c])
            total = now if total is None else total + now
        past[k] = total

    def contract(step, k):
        whole = land.at[step, k]
        pltpu.make_async_copy(whole, whole, cast_recv.at[step, k]).wait()
        total = past[k]
        for g in range(group):
            total = total + product(land[step, k, pl.ds(g * span, span)], sums[g])
        part[step, k] = total.astype(jnp.bfloat16)
        for o in range(1, ncol):
            peer = lax.rem(q + o, ncol)
            pltpu.make_async_remote_copy(
                src_ref=part.at[step, k, pl.ds(pl.multiple_of(peer * rows, rows), rows)],
                dst_ref=red.at[step, k, o - 1],
                send_sem=part_send.at[step], recv_sem=part_recv.at[step, k],
                device_id=(p, peer), device_id_type=MESH,
            ).start()
        term[k] = total

    def finish(step, row, k, right_ref, inverse, own):
        update = term[k, pl.ds(pl.multiple_of(q * rows, rows), rows)]
        arrived = red.at[step, k]
        pltpu.make_async_copy(arrived, arrived, part_recv.at[step, k]).wait()
        for o in range(ncol - 1):
            update = update + red[step, k, o].astype(jnp.float32)
        here = pl.ds(k * rows, rows)
        residual = (right_ref[row, here].astype(jnp.float32) - update).astype(jnp.bfloat16)
        own[row, here] = product(residual, inverse[row]).astype(jnp.bfloat16)

    def hand_out(l):
        place = out_hbm.at[0, l, mine]
        for o in range(1, ncol):
            pltpu.make_async_remote_copy(
                src_ref=bown.at[l], dst_ref=place,
                send_sem=out_send.at[l], recv_sem=out_recv,
                device_id=(p, lax.rem(q + o, ncol)), device_id_type=MESH,
            ).start()
        pltpu.make_async_copy(bown.at[l], place, out_recv).start()

    load_linv(0).wait()
    load_right.wait()
    fown[0] = product(right[0], linv[0]).astype(jnp.bfloat16)
    for k in range(chains):
        cast(fown, 0, 0, k)
    load_lower(0).wait()
    gather_newest(0, 0, lblk, lsrc, lcnt)

    def forward(l, _):
        load_linv(l).wait()

        @pl.when(l < last)
        def _():
            load_lower(l).wait()

        for k in range(chains):
            contract(l - 1, k)

            @pl.when(l < last)
            def _():
                keep(fstore, l - 1, l - 1, k)
                add_older(l, l, k, lblk, lsrc, lcnt, fstore)

            finish(l - 1, l, k, right, linv, fown)

            @pl.when(l < last)
            def _():
                cast(fown, l, l, k)

        @pl.when(l < last)
        def _():
            gather_newest(l, l, lblk, lsrc, lcnt)

        return 0

    lax.fori_loop(1, levels, forward, 0)

    load_uinv(last).wait()
    bown[last] = product(fown[last], uinv[last]).astype(jnp.bfloat16)
    for k in range(chains):
        cast(bown, last, last, k)
    hand_out(last)
    load_upper(last - 1).wait()
    gather_newest(last - 1, last, ublk, usrc, ucnt)
    past[...] = jnp.zeros_like(past)

    def backward(i, _):
        l = last - 1 - i
        step = last + i
        load_uinv(l).wait()

        @pl.when(l > 0)
        def _():
            load_upper(l - 1).wait()

        for k in range(chains):
            contract(step, k)

            @pl.when(l > 0)
            def _():
                keep(bstore, l + 1, step, k)
                add_older(l - 1, l, k, ublk, usrc, ucnt, bstore)

            finish(step, l, k, fown, uinv, bown)

            @pl.when(l > 0)
            def _():
                cast(bown, l, step + 1, k)

        hand_out(l)

        @pl.when(l > 0)
        def _():
            gather_newest(l - 1, l, ublk, usrc, ucnt)

        return 0

    lax.fori_loop(0, last, backward, 0)

    def drain(step, _):
        sent = red.at[step]
        pltpu.make_async_copy(sent, sent, part_send.at[step]).wait()
        for k in range(chains):
            sent = land.at[step, k, pl.ds(0, (width - 1) * rows)]
            pltpu.make_async_copy(sent, sent, cast_send.at[step]).wait()

        @pl.when(q != column)
        def _():
            one = land.at[step, 0, pl.ds(0, piece)]
            pltpu.make_async_copy(one, one, cast_send.at[step]).wait()

        return 0

    lax.fori_loop(0, 2 * last, drain, 0)
    for l in range(levels):
        sent = red.at[0]
        pltpu.make_async_copy(sent, sent, out_send.at[l]).wait()
    pltpu.make_async_copy(out_hbm.at[0], out_hbm.at[0], out_recv).wait()


def shards(right_side, lower_inverse, upper_inverse, lower_blocks, lower_sources, lower_counts,
           upper_blocks, upper_sources, upper_counts):
    width = lax.axis_size("prow")
    ncol = lax.axis_size("pcol")
    group = width // ncol
    _, levels, nrhs, sn = right_side.shape
    slots = lower_blocks.shape[2]
    piece = nrhs // ncol
    chains = 2 if piece % 32 == 0 else 1
    steps = 2 * (levels - 1)
    bf16 = jnp.bfloat16
    anywhere = pl.BlockSpec(memory_space=pl.ANY)
    scalars = pl.BlockSpec(memory_space=pltpu.SMEM)
    dma = pltpu.SemaphoreType.DMA
    return pl.pallas_call(
        functools.partial(kernel, width, ncol, chains),
        out_shape=jax.ShapeDtypeStruct(right_side.shape, bf16),
        in_specs=[anywhere, anywhere, anywhere, anywhere, scalars, scalars, anywhere, scalars, scalars],
        out_specs=anywhere,
        scratch_shapes=[
            pltpu.VMEM((levels, piece, sn), bf16),
            pltpu.VMEM((levels, sn, sn), bf16),
            pltpu.VMEM((levels, sn, sn), bf16),
            pltpu.VMEM((levels - 1, slots, sn, sn), bf16),
            pltpu.VMEM((levels - 1, slots, sn, sn), bf16),
            pltpu.VMEM((levels, piece, sn), bf16),
            pltpu.VMEM((levels, piece, sn), bf16),
            pltpu.VMEM((steps, chains, nrhs // chains, sn), bf16),
            pltpu.VMEM((chains, nrhs // chains, sn), jnp.float32),
            pltpu.VMEM((steps, chains, ncol - 1, piece // chains, sn), bf16),
            pltpu.VMEM((steps, chains, group * nrhs // chains, sn), bf16),
            pltpu.VMEM((chains, levels * group + 1, nrhs // chains, sn), bf16),
            pltpu.VMEM((chains, levels * group + 1, nrhs // chains, sn), bf16),
            pltpu.VMEM((group, sn, sn), bf16),
            pltpu.VMEM((chains, nrhs // chains, sn), jnp.float32),
            dma, dma((levels,)), dma((levels,)), dma((levels - 1,)), dma((levels - 1,)),
            dma((steps,)), dma((steps, chains)), dma((steps,)), dma((steps, chains)), dma((levels,)), dma,
        ],
        compiler_params=pltpu.CompilerParams(
            collective_id=0, has_side_effects=True, vmem_limit_bytes=60 * 1024 * 1024
        ),
        cost_estimate=pl.CostEstimate(flops=1200000000, bytes_accessed=10000000, transcendentals=0),
    )(right_side, lower_inverse, upper_inverse,
      lower_blocks, jnp.swapaxes(lower_sources, 0, 1), jnp.swapaxes(lower_counts, 1, 2),
      upper_blocks, jnp.swapaxes(upper_sources, 0, 1), jnp.swapaxes(upper_counts, 1, 2))


def solution(mesh):
    in_specs = (
        P("prow", None, None, None),
        P("prow", None, None, None),
        P("prow", None, None, None),
        P("prow", None, "pcol", None, None),
        P("prow", None, "pcol"),
        P("prow", None, "pcol"),
        P("prow", None, "pcol", None, None),
        P("prow", None, "pcol"),
        P("prow", None, "pcol"),
    )
    out_specs = P("prow", None, None, None)
    return jax.shard_map(shards, mesh=mesh, in_specs=in_specs, out_specs=out_specs, check_vma=False)
```

```python
import functools

import jax
import jax.numpy as jnp
from jax import lax
from jax.experimental import pallas as pl
from jax.experimental.pallas import tpu as pltpu
from jax.sharding import PartitionSpec as P

MESH = pl.DeviceIdType.MESH
NT = (((1,), (1,)), ((), ()))


def product(rows, matrix):
    return lax.dot_general(rows, matrix, NT, preferred_element_type=jnp.float32)


def kernel(
    width, ncol, chains,
    right_hbm, linv_hbm, uinv_hbm, lblk_hbm, lsrc, lcnt, ublk_hbm, usrc, ucnt,
    out_hbm,
    right, linv, uinv, lblk, ublk, fown, bown, part, term, red, land, fstore, bstore, sums, past,
    right_sem, linv_sem, uinv_sem, lblk_sem, ublk_sem,
    part_send, part_recv, cast_send, cast_recv, out_send, out_recv,
):
    levels, nrhs, sn = right.shape
    slots = lblk.shape[1]
    group = width // ncol
    span = nrhs // chains
    last = levels - 1
    p = lax.axis_index("prow")
    q = lax.axis_index("pcol")
    column = lax.rem(p, ncol)
    owner = q == column

    def load_lower(l):
        return pltpu.make_async_copy(lblk_hbm.at[0, l], lblk.at[l], lblk_sem.at[l])

    def load_upper(l):
        return pltpu.make_async_copy(ublk_hbm.at[0, l], ublk.at[l], ublk_sem.at[l])

    def load_linv(l):
        return pltpu.make_async_copy(linv_hbm.at[0, l], linv.at[l], linv_sem.at[l])

    def load_uinv(l):
        return pltpu.make_async_copy(uinv_hbm.at[0, l], uinv.at[l], uinv_sem.at[l])

    load_right = pltpu.make_async_copy(right_hbm.at[0], right, right_sem)
    load_linv(0).start()
    load_right.start()
    for l in range(last):
        load_lower(l).start()
        load_linv(l + 1).start()
    load_uinv(last).start()
    for l in range(last - 1, -1, -1):
        load_upper(l).start()
        load_uinv(l).start()

    barrier = pltpu.get_barrier_semaphore()

    def greet(row, c):
        pl.semaphore_signal(barrier, inc=1, device_id=(row, c), device_id_type=MESH)

    for g in range(group):
        row = q + g * ncol

        @pl.when(row != p)
        def _():
            greet(row, q)

    @pl.when(owner)
    def _():
        for o in range(1, ncol):
            greet(p, lax.rem(q + o, ncol))

    @pl.when(jnp.logical_not(owner))
    def _():
        greet(p, column)

    for k in range(chains):
        fstore[k, levels * group] = jnp.zeros((span, sn), jnp.bfloat16)
        bstore[k, levels * group] = jnp.zeros((span, sn), jnp.bfloat16)
    past[...] = jnp.zeros_like(past)

    @pl.when(owner)
    def _():
        pl.semaphore_wait(barrier, width + ncol - 2)

    @pl.when(jnp.logical_not(owner))
    def _():
        pl.semaphore_wait(barrier, 1)


    slot_rows = pl.ds(pl.multiple_of(lax.div(p, ncol) * span, span), span)

    def cast(own, l, step, k):
        piece = own.at[l, pl.ds(k * span, span)]
        place = land.at[step, k, slot_rows]
        for j in range(1, width):
            pltpu.make_async_remote_copy(
                src_ref=piece, dst_ref=place,
                send_sem=cast_send.at[step], recv_sem=cast_recv.at[step, k],
                device_id=(lax.rem(p + j, width), column), device_id_type=MESH,
            ).start()
        pltpu.make_async_copy(piece, place, cast_recv.at[step, k]).start()

    def keep(store, l, step, k):
        for g in range(group):
            store[k, l * group + g] = land[step, k, pl.ds(g * span, span)]

    def gather_newest(at, newest, blocks, sources, counts):
        count = counts[0, 0, at]
        weights = []
        for c in range(slots):
            source = sources[at, 0, c]
            fits = jnp.logical_and(c < count, lax.div(source, width) == newest)
            place = jnp.where(fits, lax.div(lax.rem(source, width), ncol), group)
            weights.append([jnp.where(place == g, 1.0, 0.0).astype(jnp.float32) for g in range(group)])
        height = sn // 4
        for r in range(0, sn, height):
            total = [None] * group
            for c in range(slots):
                block = blocks[at, c, pl.ds(r, height)].astype(jnp.float32)
                for g in range(group):
                    now = block * weights[c][g]
                    total[g] = now if total[g] is None else total[g] + now
            for g in range(group):
                sums[g, pl.ds(r, height)] = total[g].astype(jnp.bfloat16)

    def add_older(at, newest, k, blocks, sources, counts, store):
        count = counts[0, 0, at]
        total = None
        for c in range(slots):
            source = sources[at, 0, c]
            level = lax.div(source, width)
            place = level * group + lax.div(lax.rem(source, width), ncol)
            fits = jnp.logical_and(c < count, level != newest)
            now = product(store[k, jnp.where(fits, place, levels * group)], blocks[at, c])
            total = now if total is None else total + now
        past[k] = total

    def contract(step, k):
        whole = land.at[step, k]
        pltpu.make_async_copy(whole, whole, cast_recv.at[step, k]).wait()
        total = past[k]
        for g in range(group):
            total = total + product(land[step, k, pl.ds(g * span, span)], sums[g])

        @pl.when(owner)
        def _():
            term[k] = total

        @pl.when(jnp.logical_not(owner))
        def _():
            part[step, k] = total.astype(jnp.bfloat16)
            pltpu.make_async_remote_copy(
                src_ref=part.at[step, k], dst_ref=red.at[step, k, lax.rem(q - column + ncol, ncol) - 1],
                send_sem=part_send.at[step], recv_sem=part_recv.at[step, k],
                device_id=(p, column), device_id_type=MESH,
            ).start()

    def finish(step, row, k, right_ref, inverse, own):
        arrived = red.at[step, k]
        pltpu.make_async_copy(arrived, arrived, part_recv.at[step, k]).wait()
        update = term[k]
        for o in range(ncol - 1):
            update = update + red[step, k, o].astype(jnp.float32)
        here = pl.ds(k * span, span)
        residual = (right_ref[row, here].astype(jnp.float32) - update).astype(jnp.bfloat16)
        own[row, here] = product(residual, inverse[row]).astype(jnp.bfloat16)

    def hand_out(l):
        for o in range(1, ncol):
            pltpu.make_async_remote_copy(
                src_ref=bown.at[l], dst_ref=out_hbm.at[0, l],
                send_sem=out_send, recv_sem=out_recv,
                device_id=(p, lax.rem(q + o, ncol)), device_id_type=MESH,
            ).start()
        pltpu.make_async_copy(bown.at[l], out_hbm.at[0, l], out_recv).start()

    load_linv(0).wait()
    load_right.wait()

    @pl.when(owner)
    def _():
        for k in range(chains):
            here = pl.ds(k * span, span)
            fown[0, here] = product(right[0, here], linv[0]).astype(jnp.bfloat16)
            cast(fown, 0, 0, k)

    load_lower(0).wait()
    gather_newest(0, 0, lblk, lsrc, lcnt)

    def forward(l, _):
        load_linv(l).wait()

        @pl.when(l < last)
        def _():
            load_lower(l).wait()

        for k in range(chains):
            contract(l - 1, k)

            @pl.when(l < last)
            def _():
                keep(fstore, l - 1, l - 1, k)
                add_older(l, l, k, lblk, lsrc, lcnt, fstore)

            @pl.when(owner)
            def _():
                finish(l - 1, l, k, right, linv, fown)

                @pl.when(l < last)
                def _():
                    cast(fown, l, l, k)

        @pl.when(l < last)
        def _():
            gather_newest(l, l, lblk, lsrc, lcnt)

        return 0

    lax.fori_loop(1, levels, forward, 0)

    load_uinv(last).wait()

    @pl.when(owner)
    def _():
        for k in range(chains):
            here = pl.ds(k * span, span)
            bown[last, here] = product(fown[last, here], uinv[last]).astype(jnp.bfloat16)
            cast(bown, last, last, k)
        hand_out(last)

    load_upper(last - 1).wait()
    gather_newest(last - 1, last, ublk, usrc, ucnt)
    past[...] = jnp.zeros_like(past)

    def backward(i, _):
        l = last - 1 - i
        step = last + i
        load_uinv(l).wait()

        @pl.when(l > 0)
        def _():
            load_upper(l - 1).wait()

        for k in range(chains):
            contract(step, k)

            @pl.when(l > 0)
            def _():
                keep(bstore, l + 1, step, k)
                add_older(l - 1, l, k, ublk, usrc, ucnt, bstore)

            @pl.when(owner)
            def _():
                finish(step, l, k, fown, uinv, bown)

                @pl.when(l > 0)
                def _():
                    cast(bown, l, step + 1, k)

        @pl.when(owner)
        def _():
            hand_out(l)

        @pl.when(l > 0)
        def _():
            gather_newest(l - 1, l, ublk, usrc, ucnt)

        return 0

    lax.fori_loop(0, last, backward, 0)

    @pl.when(owner)
    def _():
        def drain(step, _):
            sent = part.at[step]
            for j in range(1, width):
                pltpu.make_async_copy(sent, sent, cast_send.at[step]).wait()
            return 0

        lax.fori_loop(0, 2 * last, drain, 0)
        for o in range(1, ncol):
            pltpu.make_async_copy(out_hbm.at[0], out_hbm.at[0], out_send).wait()

    @pl.when(jnp.logical_not(owner))
    def _():
        def drain(step, _):
            sent = part.at[step]
            pltpu.make_async_copy(sent, sent, part_send.at[step]).wait()
            return 0

        lax.fori_loop(0, 2 * last, drain, 0)

    pltpu.make_async_copy(out_hbm.at[0], out_hbm.at[0], out_recv).wait()


def shards(right_side, lower_inverse, upper_inverse, lower_blocks, lower_sources, lower_counts,
           upper_blocks, upper_sources, upper_counts):
    width = lax.axis_size("prow")
    ncol = lax.axis_size("pcol")
    group = width // ncol
    _, levels, nrhs, sn = right_side.shape
    slots = lower_blocks.shape[2]
    chains = 2
    span = nrhs // chains
    steps = 2 * (levels - 1)
    bf16 = jnp.bfloat16
    anywhere = pl.BlockSpec(memory_space=pl.ANY)
    scalars = pl.BlockSpec(memory_space=pltpu.SMEM)
    dma = pltpu.SemaphoreType.DMA
    return pl.pallas_call(
        functools.partial(kernel, width, ncol, chains),
        out_shape=jax.ShapeDtypeStruct(right_side.shape, bf16),
        in_specs=[anywhere, anywhere, anywhere, anywhere, scalars, scalars, anywhere, scalars, scalars],
        out_specs=anywhere,
        scratch_shapes=[
            pltpu.VMEM((levels, nrhs, sn), bf16),
            pltpu.VMEM((levels, sn, sn), bf16),
            pltpu.VMEM((levels, sn, sn), bf16),
            pltpu.VMEM((levels - 1, slots, sn, sn), bf16),
            pltpu.VMEM((levels - 1, slots, sn, sn), bf16),
            pltpu.VMEM((levels, nrhs, sn), bf16),
            pltpu.VMEM((levels, nrhs, sn), bf16),
            pltpu.VMEM((steps, chains, span, sn), bf16),
            pltpu.VMEM((chains, span, sn), jnp.float32),
            pltpu.VMEM((steps, chains, ncol - 1, span, sn), bf16),
            pltpu.VMEM((steps, chains, group * span, sn), bf16),
            pltpu.VMEM((chains, levels * group + 1, span, sn), bf16),
            pltpu.VMEM((chains, levels * group + 1, span, sn), bf16),
            pltpu.VMEM((group, sn, sn), bf16),
            pltpu.VMEM((chains, span, sn), jnp.float32),
            dma, dma((levels,)), dma((levels,)), dma((levels - 1,)), dma((levels - 1,)),
            dma((steps,)), dma((steps, chains)), dma((steps,)), dma((steps, chains)), dma, dma,
        ],
        compiler_params=pltpu.CompilerParams(
            collective_id=0, has_side_effects=True, vmem_limit_bytes=60 * 1024 * 1024
        ),
        cost_estimate=pl.CostEstimate(flops=1200000000, bytes_accessed=10000000, transcendentals=0),
    )(right_side, lower_inverse, upper_inverse,
      lower_blocks, jnp.swapaxes(lower_sources, 0, 1), jnp.swapaxes(lower_counts, 1, 2),
      upper_blocks, jnp.swapaxes(upper_sources, 0, 1), jnp.swapaxes(upper_counts, 1, 2))


def solution(mesh):
    in_specs = (
        P("prow", None, None, None),
        P("prow", None, None, None),
        P("prow", None, None, None),
        P("prow", None, "pcol", None, None),
        P("prow", None, "pcol"),
        P("prow", None, "pcol"),
        P("prow", None, "pcol", None, None),
        P("prow", None, "pcol"),
        P("prow", None, "pcol"),
    )
    out_specs = P("prow", None, None, None)
    return jax.shard_map(shards, mesh=mesh, in_specs=in_specs, out_specs=out_specs, check_vma=False)
```

```python
import functools

import jax
import jax.numpy as jnp
from jax import lax
from jax.experimental import pallas as pl
from jax.experimental.pallas import tpu as pltpu
from jax.sharding import PartitionSpec as P

MESH = pl.DeviceIdType.MESH
NT = (((1,), (1,)), ((), ()))


def product(rows, matrix):
    return lax.dot_general(rows, matrix, NT, preferred_element_type=jnp.float32)


def kernel(
    width, ncol, chains,
    right_hbm, linv_hbm, uinv_hbm, lblk_hbm, lsrc, lcnt, ublk_hbm, usrc, ucnt,
    out_hbm,
    right, linv, uinv, lblk, ublk, fown, bown, part, term, red, land, fstore, bstore, sums, past,
    right_sem, linv_sem, uinv_sem, lblk_sem, ublk_sem,
    part_send, part_recv, cast_send, cast_recv, out_send, out_recv,
):
    levels, piece, sn = right.shape
    slots = lblk.shape[1]
    group = width // ncol
    nrhs = piece * ncol
    rows = piece // chains
    span = nrhs // chains
    last = levels - 1
    p = lax.axis_index("prow")
    q = lax.axis_index("pcol")
    column = lax.rem(p, ncol)
    mine = pl.ds(pl.multiple_of(q * piece, piece), piece)

    def load_lower(l):
        return pltpu.make_async_copy(lblk_hbm.at[0, l], lblk.at[l], lblk_sem.at[l])

    def load_upper(l):
        return pltpu.make_async_copy(ublk_hbm.at[0, l], ublk.at[l], ublk_sem.at[l])

    def load_linv(l):
        return pltpu.make_async_copy(linv_hbm.at[0, l], linv.at[l], linv_sem.at[l])

    def load_uinv(l):
        return pltpu.make_async_copy(uinv_hbm.at[0, l], uinv.at[l], uinv_sem.at[l])

    load_right = pltpu.make_async_copy(right_hbm.at[0, :, mine], right, right_sem)
    load_linv(0).start()
    load_right.start()
    for l in range(last):
        load_lower(l).start()
        load_linv(l + 1).start()
    load_uinv(last).start()
    for l in range(last - 1, -1, -1):
        load_upper(l).start()
        load_uinv(l).start()

    barrier = pltpu.get_barrier_semaphore()
    for o in range(1, ncol):
        pl.semaphore_signal(barrier, inc=1, device_id=(p, lax.rem(q + o, ncol)), device_id_type=MESH)
    for g in range(group):
        row = q + g * ncol

        @pl.when(row != p)
        def _():
            for c in range(ncol):
                pl.semaphore_signal(barrier, inc=1, device_id=(row, c), device_id_type=MESH)

    fstore[levels * group] = jnp.zeros((nrhs, sn), jnp.bfloat16)
    bstore[levels * group] = jnp.zeros((nrhs, sn), jnp.bfloat16)
    past[...] = jnp.zeros_like(past)
    pl.semaphore_wait(barrier, width + ncol - 2)

    slot_rows = pl.ds(pl.multiple_of(p // ncol * span + q * rows, rows), rows)

    def cast_copy(own, l, step, k, row):
        return pltpu.make_async_remote_copy(
            src_ref=own.at[l, pl.ds(k * rows, rows)], dst_ref=land.at[step, k, slot_rows],
            send_sem=cast_send.at[step], recv_sem=cast_recv.at[step, k],
            device_id=(row, column), device_id_type=MESH,
        )

    def cast(own, l, step, k):
        for j in range(1, width):
            cast_copy(own, l, step, k, lax.rem(p + j, width)).start()

        @pl.when(q != column)
        def _():
            cast_copy(own, l, step, k, p).start()

        @pl.when(q == column)
        def _():
            pltpu.make_async_copy(
                own.at[l, pl.ds(k * rows, rows)], land.at[step, k, slot_rows], cast_recv.at[step, k]
            ).start()

    def keep(store, l, step, k):
        for g in range(group):
            store[l * group + g, pl.ds(k * span, span)] = land[step, k, pl.ds(g * span, span)]

    def gather_newest(step, at, newest, blocks, sources, counts):
        count = counts[0, 0, at]
        weights = []
        for c in range(slots):
            source = sources[at, 0, c]
            fits = jnp.logical_and(c < count, lax.div(source, width) == newest)
            place = jnp.where(fits, lax.div(lax.rem(source, width), ncol), group)
            weights.append([jnp.where(place == g, 1.0, 0.0).astype(jnp.float32) for g in range(group)])
        height = sn // 4
        for r in range(0, sn, height):
            total = [None] * group
            for c in range(slots):
                block = blocks[at, c, pl.ds(r, height)].astype(jnp.float32)
                for g in range(group):
                    now = block * weights[c][g]
                    total[g] = now if total[g] is None else total[g] + now
            for g in range(group):
                sums[lax.rem(step, 2), g, pl.ds(r, height)] = total[g].astype(jnp.bfloat16)

    def add_older(at, newest, blocks, sources, counts, store):
        count = counts[0, 0, at]
        total = None
        for c in range(slots):
            source = sources[at, 0, c]
            level = lax.div(source, width)
            place = level * group + lax.div(lax.rem(source, width), ncol)
            fits = jnp.logical_and(c < count, level != newest)
            now = product(store[jnp.where(fits, place, levels * group)], blocks[at, c])
            total = now if total is None else total + now
        past[...] = total

    def contract(step, k):
        whole = land.at[step, k]
        pltpu.make_async_copy(whole, whole, cast_recv.at[step, k]).wait()
        total = past[pl.ds(k * span, span)]
        for g in range(group):
            total = total + product(land[step, k, pl.ds(g * span, span)], sums[lax.rem(step, 2), g])
        part[step, k] = total.astype(jnp.bfloat16)
        for o in range(1, ncol):
            peer = lax.rem(q + o, ncol)
            pltpu.make_async_remote_copy(
                src_ref=part.at[step, k, pl.ds(pl.multiple_of(peer * rows, rows), rows)],
                dst_ref=red.at[step, k, o - 1],
                send_sem=part_send.at[step], recv_sem=part_recv.at[step, k],
                device_id=(p, peer), device_id_type=MESH,
            ).start()
        term[k] = total

    def finish(step, row, k, right_ref, inverse, own):
        update = term[k, pl.ds(pl.multiple_of(q * rows, rows), rows)]
        arrived = red.at[step, k]
        pltpu.make_async_copy(arrived, arrived, part_recv.at[step, k]).wait()
        for o in range(ncol - 1):
            update = update + red[step, k, o].astype(jnp.float32)
        here = pl.ds(k * rows, rows)
        residual = (right_ref[row, here].astype(jnp.float32) - update).astype(jnp.bfloat16)
        own[row, here] = product(residual, inverse[row]).astype(jnp.bfloat16)

    def hand_out(l):
        place = out_hbm.at[0, l, mine]
        for o in range(1, ncol):
            pltpu.make_async_remote_copy(
                src_ref=bown.at[l], dst_ref=place,
                send_sem=out_send.at[l], recv_sem=out_recv,
                device_id=(p, lax.rem(q + o, ncol)), device_id_type=MESH,
            ).start()
        pltpu.make_async_copy(bown.at[l], place, out_recv).start()

    load_linv(0).wait()
    load_right.wait()
    fown[0] = product(right[0], linv[0]).astype(jnp.bfloat16)
    for k in range(chains):
        cast(fown, 0, 0, k)
    load_lower(0).wait()
    gather_newest(jnp.int32(0), 0, 0, lblk, lsrc, lcnt)

    def forward(l, _):
        load_linv(l).wait()

        @pl.when(l < last)
        def _():
            load_lower(l).wait()

        for k in range(chains):
            contract(l - 1, k)

            @pl.when(l < last)
            def _():
                keep(fstore, l - 1, l - 1, k)
                if k == 0:
                    gather_newest(l, l, l, lblk, lsrc, lcnt)
                if k == chains - 1:
                    add_older(l, l, lblk, lsrc, lcnt, fstore)

            finish(l - 1, l, k, right, linv, fown)

            @pl.when(l < last)
            def _():
                cast(fown, l, l, k)

        return 0

    lax.fori_loop(1, levels, forward, 0)

    load_uinv(last).wait()
    bown[last] = product(fown[last], uinv[last]).astype(jnp.bfloat16)
    for k in range(chains):
        cast(bown, last, last, k)
    hand_out(last)
    load_upper(last - 1).wait()
    gather_newest(jnp.int32(last), last - 1, last, ublk, usrc, ucnt)
    past[...] = jnp.zeros_like(past)

    def backward(i, _):
        l = last - 1 - i
        step = last + i
        load_uinv(l).wait()

        @pl.when(l > 0)
        def _():
            load_upper(l - 1).wait()

        for k in range(chains):
            contract(step, k)

            @pl.when(l > 0)
            def _():
                keep(bstore, l + 1, step, k)
                if k == 0:
                    gather_newest(step + 1, l - 1, l, ublk, usrc, ucnt)
                if k == chains - 1:
                    add_older(l - 1, l, ublk, usrc, ucnt, bstore)

            finish(step, l, k, fown, uinv, bown)

            @pl.when(l > 0)
            def _():
                cast(bown, l, step + 1, k)

        hand_out(l)

        return 0

    lax.fori_loop(0, last, backward, 0)

    def drain(step, _):
        sent = red.at[step]
        pltpu.make_async_copy(sent, sent, part_send.at[step]).wait()
        for k in range(chains):
            sent = land.at[step, k, pl.ds(0, (width - 1) * rows)]
            pltpu.make_async_copy(sent, sent, cast_send.at[step]).wait()

        @pl.when(q != column)
        def _():
            one = land.at[step, 0, pl.ds(0, piece)]
            pltpu.make_async_copy(one, one, cast_send.at[step]).wait()

        return 0

    lax.fori_loop(0, 2 * last, drain, 0)
    for l in range(levels):
        sent = red.at[0]
        pltpu.make_async_copy(sent, sent, out_send.at[l]).wait()
    pltpu.make_async_copy(out_hbm.at[0], out_hbm.at[0], out_recv).wait()


def shards(right_side, lower_inverse, upper_inverse, lower_blocks, lower_sources, lower_counts,
           upper_blocks, upper_sources, upper_counts):
    width = lax.axis_size("prow")
    ncol = lax.axis_size("pcol")
    group = width // ncol
    _, levels, nrhs, sn = right_side.shape
    slots = lower_blocks.shape[2]
    piece = nrhs // ncol
    chains = 2 if piece % 32 == 0 else 1
    steps = 2 * (levels - 1)
    bf16 = jnp.bfloat16
    anywhere = pl.BlockSpec(memory_space=pl.ANY)
    scalars = pl.BlockSpec(memory_space=pltpu.SMEM)
    dma = pltpu.SemaphoreType.DMA
    return pl.pallas_call(
        functools.partial(kernel, width, ncol, chains),
        out_shape=jax.ShapeDtypeStruct(right_side.shape, bf16),
        in_specs=[anywhere, anywhere, anywhere, anywhere, scalars, scalars, anywhere, scalars, scalars],
        out_specs=anywhere,
        scratch_shapes=[
            pltpu.VMEM((levels, piece, sn), bf16),
            pltpu.VMEM((levels, sn, sn), bf16),
            pltpu.VMEM((levels, sn, sn), bf16),
            pltpu.VMEM((levels - 1, slots, sn, sn), bf16),
            pltpu.VMEM((levels - 1, slots, sn, sn), bf16),
            pltpu.VMEM((levels, piece, sn), bf16),
            pltpu.VMEM((levels, piece, sn), bf16),
            pltpu.VMEM((steps, chains, nrhs // chains, sn), bf16),
            pltpu.VMEM((chains, nrhs // chains, sn), jnp.float32),
            pltpu.VMEM((steps, chains, ncol - 1, piece // chains, sn), bf16),
            pltpu.VMEM((steps, chains, group * nrhs // chains, sn), bf16),
            pltpu.VMEM((levels * group + 1, nrhs, sn), bf16),
            pltpu.VMEM((levels * group + 1, nrhs, sn), bf16),
            pltpu.VMEM((2, group, sn, sn), bf16),
            pltpu.VMEM((nrhs, sn), jnp.float32),
            dma, dma((levels,)), dma((levels,)), dma((levels - 1,)), dma((levels - 1,)),
            dma((steps,)), dma((steps, chains)), dma((steps,)), dma((steps, chains)), dma((levels,)), dma,
        ],
        compiler_params=pltpu.CompilerParams(
            collective_id=0, has_side_effects=True, vmem_limit_bytes=60 * 1024 * 1024
        ),
        cost_estimate=pl.CostEstimate(flops=1200000000, bytes_accessed=10000000, transcendentals=0),
    )(right_side, lower_inverse, upper_inverse,
      lower_blocks, jnp.swapaxes(lower_sources, 0, 1), jnp.swapaxes(lower_counts, 1, 2),
      upper_blocks, jnp.swapaxes(upper_sources, 0, 1), jnp.swapaxes(upper_counts, 1, 2))


def solution(mesh):
    in_specs = (
        P("prow", None, None, None),
        P("prow", None, None, None),
        P("prow", None, None, None),
        P("prow", None, "pcol", None, None),
        P("prow", None, "pcol"),
        P("prow", None, "pcol"),
        P("prow", None, "pcol", None, None),
        P("prow", None, "pcol"),
        P("prow", None, "pcol"),
    )
    out_specs = P("prow", None, None, None)
    return jax.shard_map(shards, mesh=mesh, in_specs=in_specs, out_specs=out_specs, check_vma=False)
```

```python
import functools

import jax
import jax.numpy as jnp
from jax import lax
from jax.experimental import pallas as pl
from jax.experimental.pallas import tpu as pltpu
from jax.sharding import PartitionSpec as P

MESH = pl.DeviceIdType.MESH
NT = (((1,), (1,)), ((), ()))


def product(rows, matrix):
    return lax.dot_general(rows, matrix, NT, preferred_element_type=jnp.float32)


def kernel(
    width, ncol, inner, chains,
    right_hbm, linv_hbm, uinv_hbm, lblk_hbm, lsrc, lcnt, ublk_hbm, usrc, ucnt,
    out_hbm,
    right, linv, uinv, lblk, ublk, fown, bown, part, term, red, land, fstore, bstore, sums, past,
    right_sem, linv_sem, uinv_sem, lblk_sem, ublk_sem,
    part_send, part_recv, cast_send, cast_recv, out_send, out_recv,
):
    levels, piece, sn = right.shape
    slots = lblk.shape[1]
    group = width // ncol
    nrhs = piece * ncol
    rows = piece // chains
    span = nrhs // chains
    last = levels - 1
    p = lax.axis_index("prow")
    q = lax.axis_index("pcol")
    column = lax.rem(p, ncol)
    outer = width // inner
    p_out = lax.div(p, inner)
    p_in = lax.rem(p, inner)
    mine = pl.ds(pl.multiple_of(q * piece, piece), piece)

    def load_lower(l):
        return pltpu.make_async_copy(lblk_hbm.at[0, l], lblk.at[l], lblk_sem.at[l])

    def load_upper(l):
        return pltpu.make_async_copy(ublk_hbm.at[0, l], ublk.at[l], ublk_sem.at[l])

    def load_linv(l):
        return pltpu.make_async_copy(linv_hbm.at[0, l], linv.at[l], linv_sem.at[l])

    def load_uinv(l):
        return pltpu.make_async_copy(uinv_hbm.at[0, l], uinv.at[l], uinv_sem.at[l])

    load_right = pltpu.make_async_copy(right_hbm.at[0, :, mine], right, right_sem)
    load_linv(0).start()
    load_right.start()
    for l in range(last):
        load_lower(l).start()
        load_linv(l + 1).start()
    load_uinv(last).start()
    for l in range(last - 1, -1, -1):
        load_upper(l).start()
        load_uinv(l).start()

    barrier = pltpu.get_barrier_semaphore()
    for o in range(1, ncol):
        pl.semaphore_signal(barrier, inc=1, device_id=(p, lax.rem(q + o, ncol)), device_id_type=MESH)
    for g in range(group):
        row = q + g * ncol

        @pl.when(row != p)
        def _():
            for c in range(ncol):
                pl.semaphore_signal(barrier, inc=1, device_id=(row, c), device_id_type=MESH)

    fstore[levels * group] = jnp.zeros((nrhs, sn), jnp.bfloat16)
    bstore[levels * group] = jnp.zeros((nrhs, sn), jnp.bfloat16)
    past[...] = jnp.zeros_like(past)
    pl.semaphore_wait(barrier, width + ncol - 2)

    slot_rows = pl.ds(pl.multiple_of(p // ncol * span + q * rows, rows), rows)

    low = p_out < outer // 2
    edge = jnp.where(low, p_out, outer - 1 - p_out)

    def layer(i):
        at = jnp.where(i >= edge, i + 1, i)
        return jnp.where(low, at, outer - 1 - at)

    def cast_copy(own, l, step, k, row):
        return pltpu.make_async_remote_copy(
            src_ref=own.at[l, pl.ds(k * rows, rows)], dst_ref=land.at[step, k, slot_rows],
            send_sem=cast_send.at[step], recv_sem=cast_recv.at[step, k],
            device_id=(row, column), device_id_type=MESH,
        )

    def cast(own, l, step, k):
        for i in range(outer - 2, -1, -1):
            for j in range(inner - 1, -1, -1):
                row = layer(i) * inner + lax.rem(p_in + j, inner)
                cast_copy(own, l, step, k, row).start()
        for j in range(1, inner):
            cast_copy(own, l, step, k, p_out * inner + lax.rem(p_in + j, inner)).start()

        @pl.when(q != column)
        def _():
            cast_copy(own, l, step, k, p).start()

        @pl.when(q == column)
        def _():
            pltpu.make_async_copy(
                own.at[l, pl.ds(k * rows, rows)], land.at[step, k, slot_rows], cast_recv.at[step, k]
            ).start()

    def keep(store, l, step):
        for k in range(chains):
            for g in range(group):
                store[l * group + g, pl.ds(k * span, span)] = land[step, k, pl.ds(g * span, span)]

    def gather_newest(at, newest, blocks, sources, counts):
        count = counts[0, 0, at]
        weights = []
        for c in range(slots):
            source = sources[at, 0, c]
            fits = jnp.logical_and(c < count, lax.div(source, width) == newest)
            place = jnp.where(fits, lax.div(lax.rem(source, width), ncol), group)
            weights.append([jnp.where(place == g, 1.0, 0.0).astype(jnp.float32) for g in range(group)])
        height = sn // 4
        for r in range(0, sn, height):
            total = [None] * group
            for c in range(slots):
                block = blocks[at, c, pl.ds(r, height)].astype(jnp.float32)
                for g in range(group):
                    now = block * weights[c][g]
                    total[g] = now if total[g] is None else total[g] + now
            for g in range(group):
                sums[g, pl.ds(r, height)] = total[g].astype(jnp.bfloat16)

    def add_older(at, newest, blocks, sources, counts, store):
        count = counts[0, 0, at]
        total = None
        for c in range(slots):
            source = sources[at, 0, c]
            level = lax.div(source, width)
            place = level * group + lax.div(lax.rem(source, width), ncol)
            fits = jnp.logical_and(c < count, level != newest)
            now = product(store[jnp.where(fits, place, levels * group)], blocks[at, c])
            total = now if total is None else total + now
        past[...] = total

    def contract(step, k):
        whole = land.at[step, k]
        pltpu.make_async_copy(whole, whole, cast_recv.at[step, k]).wait()
        total = past[pl.ds(k * span, span)]
        for g in range(group):
            total = total + product(land[step, k, pl.ds(g * span, span)], sums[g])
        part[step, k] = total.astype(jnp.bfloat16)
        for o in sorted(range(1, ncol), key=lambda o: -min(o, ncol - o)):
            peer = lax.rem(q + o, ncol)
            pltpu.make_async_remote_copy(
                src_ref=part.at[step, k, pl.ds(pl.multiple_of(peer * rows, rows), rows)],
                dst_ref=red.at[step, k, o - 1],
                send_sem=part_send.at[step], recv_sem=part_recv.at[step, k],
                device_id=(p, peer), device_id_type=MESH,
            ).start()
        term[k] = total

    def finish(step, row, k, right_ref, inverse, own):
        update = term[k, pl.ds(pl.multiple_of(q * rows, rows), rows)]
        arrived = red.at[step, k]
        pltpu.make_async_copy(arrived, arrived, part_recv.at[step, k]).wait()
        for o in range(ncol - 1):
            update = update + red[step, k, o].astype(jnp.float32)
        here = pl.ds(k * rows, rows)
        residual = (right_ref[row, here].astype(jnp.float32) - update).astype(jnp.bfloat16)
        own[row, here] = product(residual, inverse[row]).astype(jnp.bfloat16)

    def hand_out(l):
        place = out_hbm.at[0, l, mine]
        for o in range(1, ncol):
            pltpu.make_async_remote_copy(
                src_ref=bown.at[l], dst_ref=place,
                send_sem=out_send.at[l], recv_sem=out_recv,
                device_id=(p, lax.rem(q + o, ncol)), device_id_type=MESH,
            ).start()
        pltpu.make_async_copy(bown.at[l], place, out_recv).start()

    load_linv(0).wait()
    load_right.wait()
    fown[0] = product(right[0], linv[0]).astype(jnp.bfloat16)
    for k in range(chains):
        cast(fown, 0, 0, k)
    load_lower(0).wait()
    gather_newest(0, 0, lblk, lsrc, lcnt)

    def forward(l, _):
        for k in range(chains):
            contract(l - 1, k)

        @pl.when(l < last)
        def _():
            load_lower(l).wait()
            gather_newest(l, l, lblk, lsrc, lcnt)
            keep(fstore, l - 1, l - 1)

        load_linv(l).wait()
        for k in range(chains):
            finish(l - 1, l, k, right, linv, fown)

            @pl.when(l < last)
            def _():
                cast(fown, l, l, k)

        @pl.when(l < last)
        def _():
            add_older(l, l, lblk, lsrc, lcnt, fstore)

        return 0

    lax.fori_loop(1, levels, forward, 0)

    load_uinv(last).wait()
    bown[last] = product(fown[last], uinv[last]).astype(jnp.bfloat16)
    for k in range(chains):
        cast(bown, last, last, k)
    hand_out(last)
    load_upper(last - 1).wait()
    gather_newest(last - 1, last, ublk, usrc, ucnt)
    past[...] = jnp.zeros_like(past)

    def backward(i, _):
        l = last - 1 - i
        step = last + i
        for k in range(chains):
            contract(step, k)

        @pl.when(l > 0)
        def _():
            load_upper(l - 1).wait()
            gather_newest(l - 1, l, ublk, usrc, ucnt)
            keep(bstore, l + 1, step)

        load_uinv(l).wait()
        for k in range(chains):
            finish(step, l, k, fown, uinv, bown)

            @pl.when(l > 0)
            def _():
                cast(bown, l, step + 1, k)

        hand_out(l)

        @pl.when(l > 0)
        def _():
            add_older(l - 1, l, ublk, usrc, ucnt, bstore)

        return 0

    lax.fori_loop(0, last, backward, 0)

    def drain(step, _):
        sent = red.at[step]
        pltpu.make_async_copy(sent, sent, part_send.at[step]).wait()
        for k in range(chains):
            sent = land.at[step, k, pl.ds(0, (width - 1) * rows)]
            pltpu.make_async_copy(sent, sent, cast_send.at[step]).wait()

        @pl.when(q != column)
        def _():
            one = land.at[step, 0, pl.ds(0, piece)]
            pltpu.make_async_copy(one, one, cast_send.at[step]).wait()

        return 0

    lax.fori_loop(0, 2 * last, drain, 0)
    for l in range(levels):
        sent = red.at[0]
        pltpu.make_async_copy(sent, sent, out_send.at[l]).wait()
    pltpu.make_async_copy(out_hbm.at[0], out_hbm.at[0], out_recv).wait()


def shards(right_side, lower_inverse, upper_inverse, lower_blocks, lower_sources, lower_counts,
           upper_blocks, upper_sources, upper_counts):
    width = lax.axis_size("prow")
    ncol = lax.axis_size("pcol")
    group = width // ncol
    _, levels, nrhs, sn = right_side.shape
    slots = lower_blocks.shape[2]
    piece = nrhs // ncol
    chains = 2 if piece % 32 == 0 else 1
    inner = 1
    while inner * inner * 4 <= width:
        inner *= 2
    steps = 2 * (levels - 1)
    bf16 = jnp.bfloat16
    anywhere = pl.BlockSpec(memory_space=pl.ANY)
    scalars = pl.BlockSpec(memory_space=pltpu.SMEM)
    dma = pltpu.SemaphoreType.DMA
    return pl.pallas_call(
        functools.partial(kernel, width, ncol, inner, chains),
        out_shape=jax.ShapeDtypeStruct(right_side.shape, bf16),
        in_specs=[anywhere, anywhere, anywhere, anywhere, scalars, scalars, anywhere, scalars, scalars],
        out_specs=anywhere,
        scratch_shapes=[
            pltpu.VMEM((levels, piece, sn), bf16),
            pltpu.VMEM((levels, sn, sn), bf16),
            pltpu.VMEM((levels, sn, sn), bf16),
            pltpu.VMEM((levels - 1, slots, sn, sn), bf16),
            pltpu.VMEM((levels - 1, slots, sn, sn), bf16),
            pltpu.VMEM((levels, piece, sn), bf16),
            pltpu.VMEM((levels, piece, sn), bf16),
            pltpu.VMEM((steps, chains, nrhs // chains, sn), bf16),
            pltpu.VMEM((chains, nrhs // chains, sn), jnp.float32),
            pltpu.VMEM((steps, chains, ncol - 1, piece // chains, sn), bf16),
            pltpu.VMEM((steps, chains, group * nrhs // chains, sn), bf16),
            pltpu.VMEM((levels * group + 1, nrhs, sn), bf16),
            pltpu.VMEM((levels * group + 1, nrhs, sn), bf16),
            pltpu.VMEM((group, sn, sn), bf16),
            pltpu.VMEM((nrhs, sn), jnp.float32),
            dma, dma((levels,)), dma((levels,)), dma((levels - 1,)), dma((levels - 1,)),
            dma((steps,)), dma((steps, chains)), dma((steps,)), dma((steps, chains)), dma((levels,)), dma,
        ],
        compiler_params=pltpu.CompilerParams(
            collective_id=0, has_side_effects=True, vmem_limit_bytes=60 * 1024 * 1024
        ),
        cost_estimate=pl.CostEstimate(flops=1200000000, bytes_accessed=10000000, transcendentals=0),
    )(right_side, lower_inverse, upper_inverse,
      lower_blocks, jnp.swapaxes(lower_sources, 0, 1), jnp.swapaxes(lower_counts, 1, 2),
      upper_blocks, jnp.swapaxes(upper_sources, 0, 1), jnp.swapaxes(upper_counts, 1, 2))


def solution(mesh):
    in_specs = (
        P("prow", None, None, None),
        P("prow", None, None, None),
        P("prow", None, None, None),
        P("prow", None, "pcol", None, None),
        P("prow", None, "pcol"),
        P("prow", None, "pcol"),
        P("prow", None, "pcol", None, None),
        P("prow", None, "pcol"),
        P("prow", None, "pcol"),
    )
    out_specs = P("prow", None, None, None)
    return jax.shard_map(shards, mesh=mesh, in_specs=in_specs, out_specs=out_specs, check_vma=False)
```

```python
import functools

import jax
import jax.numpy as jnp
from jax import lax
from jax.experimental import pallas as pl
from jax.experimental.pallas import tpu as pltpu
from jax.sharding import PartitionSpec as P

MESH = pl.DeviceIdType.MESH
NT = (((1,), (1,)), ((), ()))


def product(rows, matrix):
    return lax.dot_general(rows, matrix, NT, preferred_element_type=jnp.float32)


def kernel(
    width, ncol, chains,
    right_hbm, linv_hbm, uinv_hbm, lblk_hbm, lsrc, lcnt, ublk_hbm, usrc, ucnt,
    out_hbm,
    right, linv, uinv, lblk, ublk, fown, bown, part, term, red, land, fstore, bstore, sums, past,
    right_sem, linv_sem, uinv_sem, lblk_sem, ublk_sem,
    part_send, part_recv, cast_send, cast_recv, out_send, out_recv,
):
    levels, piece, sn = right.shape
    slots = lblk.shape[1]
    group = width // ncol
    nrhs = piece * ncol
    rows = piece // chains
    span = nrhs // chains
    last = levels - 1
    p = lax.axis_index("prow")
    q = lax.axis_index("pcol")
    column = lax.rem(p, ncol)
    mine = pl.ds(pl.multiple_of(q * piece, piece), piece)

    def load_lower(l):
        return pltpu.make_async_copy(lblk_hbm.at[0, l], lblk.at[l], lblk_sem.at[l])

    def load_upper(l):
        return pltpu.make_async_copy(ublk_hbm.at[0, l], ublk.at[l], ublk_sem.at[l])

    def load_linv(l):
        return pltpu.make_async_copy(linv_hbm.at[0, l], linv.at[l], linv_sem.at[l])

    def load_uinv(l):
        return pltpu.make_async_copy(uinv_hbm.at[0, l], uinv.at[l], uinv_sem.at[l])

    load_right = pltpu.make_async_copy(right_hbm.at[0, :, mine], right, right_sem)
    load_linv(0).start()
    load_right.start()
    for l in range(last):
        load_lower(l).start()
        load_linv(l + 1).start()
    load_uinv(last).start()
    for l in range(last - 1, -1, -1):
        load_upper(l).start()
        load_uinv(l).start()

    barrier = pltpu.get_barrier_semaphore()
    for o in range(1, ncol):
        pl.semaphore_signal(barrier, inc=1, device_id=(p, lax.rem(q + o, ncol)), device_id_type=MESH)
    for g in range(group):
        row = q + g * ncol

        @pl.when(row != p)
        def _():
            for c in range(ncol):
                pl.semaphore_signal(barrier, inc=1, device_id=(row, c), device_id_type=MESH)

    fstore[levels * group] = jnp.zeros((nrhs, sn), jnp.bfloat16)
    bstore[levels * group] = jnp.zeros((nrhs, sn), jnp.bfloat16)
    past[...] = jnp.zeros_like(past)
    pl.semaphore_wait(barrier, width + ncol - 2)

    slot_rows = pl.ds(pl.multiple_of(p // ncol * span + q * rows, rows), rows)

    def cast_copy(own, l, step, k, row):
        return pltpu.make_async_remote_copy(
            src_ref=own.at[l, pl.ds(k * rows, rows)], dst_ref=land.at[step, k, slot_rows],
            send_sem=cast_send.at[step], recv_sem=cast_recv.at[step, k],
            device_id=(row, column), device_id_type=MESH,
        )

    def cast(own, l, step, k):
        for j in range(1, width):
            cast_copy(own, l, step, k, lax.rem(p + j, width)).start()

        @pl.when(q != column)
        def _():
            cast_copy(own, l, step, k, p).start()

        @pl.when(q == column)
        def _():
            pltpu.make_async_copy(
                own.at[l, pl.ds(k * rows, rows)], land.at[step, k, slot_rows], cast_recv.at[step, k]
            ).start()

    def keep(store, l, step):
        for k in range(chains):
            for g in range(group):
                store[l * group + g, pl.ds(k * span, span)] = land[step, k, pl.ds(g * span, span)]

    def gather_newest(at, newest, blocks, sources, counts):
        count = counts[0, 0, at]
        weights = []
        for c in range(slots):
            source = sources[at, 0, c]
            fits = jnp.logical_and(c < count, lax.div(source, width) == newest)
            place = jnp.where(fits, lax.div(lax.rem(source, width), ncol), group)
            weights.append([jnp.where(place == g, 1.0, 0.0).astype(jnp.float32) for g in range(group)])
        height = sn // 4
        for r in range(0, sn, height):
            total = [None] * group
            for c in range(slots):
                block = blocks[at, c, pl.ds(r, height)].astype(jnp.float32)
                for g in range(group):
                    now = block * weights[c][g]
                    total[g] = now if total[g] is None else total[g] + now
            for g in range(group):
                sums[g, pl.ds(r, height)] = total[g].astype(jnp.bfloat16)

    def add_older(at, newest, blocks, sources, counts, store):
        count = counts[0, 0, at]
        total = None
        for c in range(slots):
            source = sources[at, 0, c]
            level = lax.div(source, width)
            place = level * group + lax.div(lax.rem(source, width), ncol)
            fits = jnp.logical_and(c < count, level != newest)
            now = product(store[jnp.where(fits, place, levels * group)], blocks[at, c])
            total = now if total is None else total + now
        past[...] = total

    def contract(step, k):
        whole = land.at[step, k]
        pltpu.make_async_copy(whole, whole, cast_recv.at[step, k]).wait()
        total = past[pl.ds(k * span, span)]
        for g in range(group):
            total = total + product(land[step, k, pl.ds(g * span, span)], sums[g])
        part[step, k] = total.astype(jnp.bfloat16)
        for o in range(1, ncol):
            peer = lax.rem(q + o, ncol)
            pltpu.make_async_remote_copy(
                src_ref=part.at[step, k, pl.ds(pl.multiple_of(peer * rows, rows), rows)],
                dst_ref=red.at[step, k, o - 1],
                send_sem=part_send.at[step], recv_sem=part_recv.at[step, k],
                device_id=(p, peer), device_id_type=MESH,
            ).start()
        term[k] = total

    def finish(step, row, k, right_ref, inverse, own):
        update = term[k, pl.ds(pl.multiple_of(q * rows, rows), rows)]
        arrived = red.at[step, k]
        pltpu.make_async_copy(arrived, arrived, part_recv.at[step, k]).wait()
        for o in range(ncol - 1):
            update = update + red[step, k, o].astype(jnp.float32)
        here = pl.ds(k * rows, rows)
        residual = (right_ref[row, here].astype(jnp.float32) - update).astype(jnp.bfloat16)
        own[row, here] = product(residual, inverse[row]).astype(jnp.bfloat16)

    def hand_out(l):
        place = out_hbm.at[0, l, mine]
        for o in range(1, ncol):
            pltpu.make_async_remote_copy(
                src_ref=bown.at[l], dst_ref=place,
                send_sem=out_send.at[l], recv_sem=out_recv,
                device_id=(p, lax.rem(q + o, ncol)), device_id_type=MESH,
            ).start()
        pltpu.make_async_copy(bown.at[l], place, out_recv).start()

    load_linv(0).wait()
    load_right.wait()
    fown[0] = product(right[0], linv[0]).astype(jnp.bfloat16)
    for k in range(chains):
        cast(fown, 0, 0, k)
    load_lower(0).wait()
    gather_newest(0, 0, lblk, lsrc, lcnt)

    def forward(l, _):
        for k in range(chains):
            contract(l - 1, k)

        @pl.when(l < last)
        def _():
            load_lower(l).wait()
            gather_newest(l, l, lblk, lsrc, lcnt)
            keep(fstore, l - 1, l - 1)

        load_linv(l).wait()
        for k in range(chains):
            finish(l - 1, l, k, right, linv, fown)

            @pl.when(l < last)
            def _():
                cast(fown, l, l, k)

        @pl.when(l < last)
        def _():
            add_older(l, l, lblk, lsrc, lcnt, fstore)

        return 0

    lax.fori_loop(1, levels, forward, 0)

    load_uinv(last).wait()
    bown[last] = product(fown[last], uinv[last]).astype(jnp.bfloat16)
    for k in range(chains):
        cast(bown, last, last, k)
    hand_out(last)
    load_upper(last - 1).wait()
    gather_newest(last - 1, last, ublk, usrc, ucnt)
    past[...] = jnp.zeros_like(past)

    def backward(i, _):
        l = last - 1 - i
        step = last + i
        for k in range(chains):
            contract(step, k)

        @pl.when(l > 0)
        def _():
            load_upper(l - 1).wait()
            gather_newest(l - 1, l, ublk, usrc, ucnt)
            keep(bstore, l + 1, step)

        load_uinv(l).wait()
        for k in range(chains):
            finish(step, l, k, fown, uinv, bown)

            @pl.when(l > 0)
            def _():
                cast(bown, l, step + 1, k)

        hand_out(l)

        @pl.when(l > 0)
        def _():
            add_older(l - 1, l, ublk, usrc, ucnt, bstore)

        return 0

    lax.fori_loop(0, last, backward, 0)

    def drain(step, _):
        sent = red.at[step]
        pltpu.make_async_copy(sent, sent, part_send.at[step]).wait()
        for k in range(chains):
            sent = land.at[step, k, pl.ds(0, (width - 1) * rows)]
            pltpu.make_async_copy(sent, sent, cast_send.at[step]).wait()

        @pl.when(q != column)
        def _():
            one = land.at[step, 0, pl.ds(0, piece)]
            pltpu.make_async_copy(one, one, cast_send.at[step]).wait()

        return 0

    lax.fori_loop(0, 2 * last, drain, 0)
    for l in range(levels):
        sent = red.at[0]
        pltpu.make_async_copy(sent, sent, out_send.at[l]).wait()
    pltpu.make_async_copy(out_hbm.at[0], out_hbm.at[0], out_recv).wait()


def shards(right_side, lower_inverse, upper_inverse, lower_blocks, lower_sources, lower_counts,
           upper_blocks, upper_sources, upper_counts):
    width = lax.axis_size("prow")
    ncol = lax.axis_size("pcol")
    group = width // ncol
    _, levels, nrhs, sn = right_side.shape
    slots = lower_blocks.shape[2]
    piece = nrhs // ncol
    chains = 1
    steps = 2 * (levels - 1)
    bf16 = jnp.bfloat16
    anywhere = pl.BlockSpec(memory_space=pl.ANY)
    scalars = pl.BlockSpec(memory_space=pltpu.SMEM)
    dma = pltpu.SemaphoreType.DMA
    return pl.pallas_call(
        functools.partial(kernel, width, ncol, chains),
        out_shape=jax.ShapeDtypeStruct(right_side.shape, bf16),
        in_specs=[anywhere, anywhere, anywhere, anywhere, scalars, scalars, anywhere, scalars, scalars],
        out_specs=anywhere,
        scratch_shapes=[
            pltpu.VMEM((levels, piece, sn), bf16),
            pltpu.VMEM((levels, sn, sn), bf16),
            pltpu.VMEM((levels, sn, sn), bf16),
            pltpu.VMEM((levels - 1, slots, sn, sn), bf16),
            pltpu.VMEM((levels - 1, slots, sn, sn), bf16),
            pltpu.VMEM((levels, piece, sn), bf16),
            pltpu.VMEM((levels, piece, sn), bf16),
            pltpu.VMEM((steps, chains, nrhs // chains, sn), bf16),
            pltpu.VMEM((chains, nrhs // chains, sn), jnp.float32),
            pltpu.VMEM((steps, chains, ncol - 1, piece // chains, sn), bf16),
            pltpu.VMEM((steps, chains, group * nrhs // chains, sn), bf16),
            pltpu.VMEM((levels * group + 1, nrhs, sn), bf16),
            pltpu.VMEM((levels * group + 1, nrhs, sn), bf16),
            pltpu.VMEM((group, sn, sn), bf16),
            pltpu.VMEM((nrhs, sn), jnp.float32),
            dma, dma((levels,)), dma((levels,)), dma((levels - 1,)), dma((levels - 1,)),
            dma((steps,)), dma((steps, chains)), dma((steps,)), dma((steps, chains)), dma((levels,)), dma,
        ],
        compiler_params=pltpu.CompilerParams(
            collective_id=0, has_side_effects=True, vmem_limit_bytes=60 * 1024 * 1024
        ),
        cost_estimate=pl.CostEstimate(flops=1200000000, bytes_accessed=10000000, transcendentals=0),
    )(right_side, lower_inverse, upper_inverse,
      lower_blocks, jnp.swapaxes(lower_sources, 0, 1), jnp.swapaxes(lower_counts, 1, 2),
      upper_blocks, jnp.swapaxes(upper_sources, 0, 1), jnp.swapaxes(upper_counts, 1, 2))


def solution(mesh):
    in_specs = (
        P("prow", None, None, None),
        P("prow", None, None, None),
        P("prow", None, None, None),
        P("prow", None, "pcol", None, None),
        P("prow", None, "pcol"),
        P("prow", None, "pcol"),
        P("prow", None, "pcol", None, None),
        P("prow", None, "pcol"),
        P("prow", None, "pcol"),
    )
    out_specs = P("prow", None, None, None)
    return jax.shard_map(shards, mesh=mesh, in_specs=in_specs, out_specs=out_specs, check_vma=False)
```
